32 devices in a mesh: groups: 2 (over x), owner: 16 (over z, y, core).
Axes of the slice: x: 2, y: 2, z: 4, core: 2. Of those that a mesh axis runs over, the one named last changes fastest.
Arguments:
- embeds: bfloat16 [16384, 768], P(('groups', 'owner')), parts along dimension 0, may hold values from -6 to 6
- clusters: int32 [16384], P(('groups', 'owner')), parts along dimension 0, may hold values from 0 to 17, as said below
- ranks: int32 [16384], P(('groups', 'owner')), parts along dimension 0, may hold values from 0 to 4095
Outputs:
- maxima: float32 [16384], P(('groups', 'owner')), parts along dimension 0
The draws below stay inside these ranges and needn't reach their ends.
There are 2 independent parts, one for each index of `groups`. The reference program is written for one: setup_inputs(seed, part) draws one part's arguments, and reference() takes and returns one part's arrays. A program takes and returns all parts, laid end to end along the dimension named above; each array names one. Nothing has to cross between parts.
Inputs may be any that keep to these rules, and one draw needn't show every extreme that they name: A cluster c below 16 is small and all its rows go to device c of owner; a cluster c of 16 or more is large and its row with rank r goes to device 8 * (c - 16) + r % 8. Of the rows of one device at most 64 go to one device. In every draw one device receives exactly 64 rows from every device, exactly half of them in large clusters.
All inputs are finite; a program needn't handle non-finite values.
Results may differ from the reference program's by a relative error of at most 0.0014.
Values may be sent and summed in bfloat16 or wider, within the bound.
No kernel may reach another device: no remote copies, remote signals or barrier semaphores. Data moves between devices by JAX's collectives and lax.ppermute only.
A program may use at most 64 MiB of HBM per device.

```python
import math
import jax
import jax.numpy as jnp
from jax import lax

D = 768
ROWS_DEV = 512
CAP = 64
ROWS = 8192
RANKS = 4096
N_OWNER = 16


def layout_rows(key):
    key = jax.random.fold_in(key, 11)
    first, second, third, fourth = jax.random.split(key, 4)
    heavy = jax.random.randint(first, (), 0, N_OWNER)
    slot_owner = jnp.arange(N_OWNER * CAP, dtype=jnp.int32) // CAP

    def one_source(sub_key):
        left_key, right_key = jax.random.split(sub_key)
        order = jax.random.permutation(left_key, N_OWNER * CAP).astype(jnp.int32)
        score = jnp.where(slot_owner == heavy, -1, order)
        picked = slot_owner[jnp.argsort(score, stable=True)[:ROWS_DEV]]
        picked = picked[jax.random.permutation(right_key, ROWS_DEV)]
        index = jnp.arange(ROWS_DEV, dtype=jnp.int32)
        before = (picked[:, None] == picked[None, :]) & (index[:, None] > index[None, :])
        ordinal = jnp.sum(before.astype(jnp.int32), axis=1)
        return (picked, ordinal)
    target, ordinal = jax.vmap(one_source)(jax.random.split(second, N_OWNER))
    target = target.reshape(ROWS)
    ordinal = ordinal.reshape(ROWS)
    big = ordinal % 2 == 0
    cluster = jnp.where(big, N_OWNER + target // 8, target)
    coarse = jax.random.randint(third, (ROWS,), 0, RANKS // 8)
    drawn = jax.random.randint(fourth, (ROWS,), 0, RANKS)
    rank = jnp.where(big, 8 * coarse + target % 8, drawn)
    return (cluster.astype(jnp.int32), rank.astype(jnp.int32))


def draw_clusters(key, part):
    cluster, rank = layout_rows(key)
    return cluster


def draw_ranks(key, part):
    cluster, rank = layout_rows(key)
    return rank


def levels(own_key, shape, pieces, least, high):
    factor_of, own = 1.0, jax.random.fold_in(own_key, 6)
    for axis_at, shards_of in pieces:
        draws = jnp.exp(jax.random.uniform(jax.random.fold_in(own, axis_at), (shards_of,), jnp.float32, least / len(pieces), high / len(pieces)))
        factor_of = factor_of * jnp.repeat(draws, shape[axis_at] // shards_of).reshape([-1 if axis == axis_at else 1 for axis in range(len(shape))])
    return factor_of


def centred(stream_key, dims, deviation, most, shards=(), kind=jnp.bfloat16):
    drawn = deviation * jax.random.normal(stream_key, dims, jnp.float32)
    if shards:
        drawn = drawn * levels(stream_key, dims, shards, -0.22, 0.18)
    return jnp.clip(drawn, -most, most).astype(kind)


def setup_inputs(seed: int = 0, part: int = 0) -> dict:
    key_of = jax.random.split(jax.random.key(seed), 4)
    own_keys = jax.random.split(jax.random.fold_in(key_of[3], part), 4)
    return {
        "embeds": centred(own_keys[0], (ROWS, D), 1.0, 6.0, ((0, 16),)),
        "clusters": draw_clusters(jax.random.fold_in(jax.random.fold_in(key_of[3], part), 71), part),
        "ranks": draw_ranks(jax.random.fold_in(jax.random.fold_in(key_of[3], part), 71), part),
    }


def reference(embeds, clusters, ranks):
    values = embeds.astype(jnp.float32)
    unit = (values * lax.rsqrt(lax.optimization_barrier(jnp.sum(values * values, axis=1, keepdims=True)) + 1e-06)).astype(jnp.bfloat16)
    block_rows = math.gcd(ROWS, 512)
    count = ROWS // block_rows

    def one_block(start_block):
        start = (start_block * block_rows).astype(jnp.int32)
        query = lax.dynamic_slice_in_dim(unit, start, block_rows, 0)
        query_cluster = lax.dynamic_slice_in_dim(clusters, start, block_rows, 0)
        query_rank = lax.dynamic_slice_in_dim(ranks, start, block_rows, 0)
        scores = jnp.dot(query, unit.T, preferred_element_type=jnp.float32)
        allowed = (clusters[None, :] == query_cluster[:, None]) & (ranks[None, :] < query_rank[:, None])
        return lax.optimization_barrier(jnp.max(jnp.where(allowed, scores, jnp.float32(-1.0)), axis=1))
    result = lax.map(one_block, jnp.arange(count, dtype=jnp.int32))
    return result.reshape(ROWS)
```

```python
import functools

import jax
import jax.numpy as jnp
from jax import lax
from jax.experimental import pallas as pl
from jax.experimental.pallas import tpu as pltpu
from jax.sharding import PartitionSpec as P

OWNERS = 16
CHIPS = 8
HOMES = (2, 3, 4, 5)
BLOCK = 160
CAP = 156
META = 16
VMEM_LIMIT = 48 * 1024 * 1024
NT = (((1,), (1,)), ((), ()))


def is_home(chip):
    return (chip >= HOMES[0]) & (chip <= HOMES[-1])


def pack_kernel(x_ref, cluster_ref, rank_ref, *outs):
    slot_ref = outs[CHIPS]
    chip = lax.axis_index("owner") // 2
    values = x_ref[...].astype(jnp.float32)
    unit = (values * lax.rsqrt(jnp.sum(values * values, axis=1, keepdims=True) + 1e-06)).astype(
        jnp.bfloat16
    )
    rows, width = unit.shape
    cluster = cluster_ref[...]
    rank = rank_ref[...]
    home = jnp.where(
        cluster < OWNERS // 2,
        3,
        jnp.where(cluster < OWNERS, 4, jnp.where(cluster == OWNERS, 2, 5)),
    )
    number = lax.broadcasted_iota(jnp.int32, (CHIPS, rows), 0)
    member = number == (home ^ chip)
    upper = (
        lax.broadcasted_iota(jnp.int32, (rows, rows), 0)
        < lax.broadcasted_iota(jnp.int32, (rows, rows), 1)
    ).astype(jnp.float32).astype(jnp.bfloat16)
    before = jnp.dot(
        member.astype(jnp.float32).astype(jnp.bfloat16), upper, preferred_element_type=jnp.float32
    )
    slot = jnp.where(member, before.astype(jnp.int32), -1)
    slot_ref[...] = slot
    over = (jnp.max(slot) >= CAP).astype(jnp.float32)
    line = lax.broadcasted_iota(jnp.int32, (META, rows), 0)
    first = META - (BLOCK - CAP)
    meta = jnp.where(
        line == first,
        cluster + 1,
        jnp.where(line == first + 1, rank >> 6, jnp.where(line == first + 2, rank & 63, 0)),
    )
    meta = meta.astype(jnp.float32).astype(jnp.bfloat16)
    for k in range(CHIPS):

        @pl.when(is_home(chip ^ k))
        def _():
            place = lax.broadcasted_iota(jnp.int32, (256, rows), 0)
            hot = ((place == slot[k : k + 1]) & (place < CAP)).astype(jnp.float32)
            hot = hot.astype(jnp.bfloat16)
            block = jnp.dot(hot[:BLOCK], unit, preferred_element_type=jnp.float32)
            outs[k][...] = block.astype(jnp.bfloat16)
            tail = lax.dot_general(meta, hot, NT, preferred_element_type=jnp.float32)
            row = lax.broadcasted_iota(jnp.int32, (META, 256), 0)
            tail = jnp.where(row == META - 1, over, tail)
            tail = jnp.where(row >= first, tail, block[BLOCK - META :, :256])
            outs[k][BLOCK - META :, :256] = tail.astype(jnp.bfloat16)


def compare_kernel(*refs):
    blocks = refs[: 2 * CHIPS]
    out_ref, keys, codes, sems = refs[2 * CHIPS :]
    me = lax.axis_index("owner")
    chip = me // 2
    core = me % 2

    @pl.when(is_home(chip))
    def _():
        copies = [
            pltpu.make_async_copy(ref, keys.at[pl.ds(n * BLOCK, BLOCK)], sems.at[n])
            for n, ref in enumerate(blocks)
        ]
        for copy in copies:
            copy.start()
        for copy in copies:
            copy.wait()
        eye = (
            lax.broadcasted_iota(jnp.int32, (BLOCK, 256), 0)
            == lax.broadcasted_iota(jnp.int32, (BLOCK, 256), 1)
        ).astype(jnp.float32).astype(jnp.bfloat16)
        lane = lax.broadcasted_iota(jnp.int32, (1, META), 1)
        first = META - (BLOCK - CAP)
        scale = jnp.where(
            lane == first, 4096.0, jnp.where(lane == first + 1, 64.0, jnp.where(lane == first + 2, 1.0, 0.0))
        )
        over = jnp.zeros((1, 128), jnp.float32)
        for n in range(2 * CHIPS):
            meta = keys[(n + 1) * BLOCK - META : (n + 1) * BLOCK, :256]
            over = jnp.maximum(over, meta[META - 1 :, :128].astype(jnp.float32))
            columns = lax.dot_general(eye, meta, NT, preferred_element_type=jnp.float32)
            code = jnp.sum(columns * scale, axis=1, keepdims=True)
            codes[n * BLOCK : (n + 1) * BLOCK] = jnp.broadcast_to(code, (BLOCK, 128))
        over = jnp.max(over)
        queries = CHIPS * BLOCK
        step = 2 * queries // 4
        found = []
        for t in range(queries // 256):
            query = keys[t * 256 : (t + 1) * 256]
            top = jnp.transpose(codes[t * 256 : (t + 1) * 256])[:1]
            base = jnp.floor(top * (1.0 / 4096.0)) * 4096.0
            best = jnp.full((8, 256), -1.0, jnp.float32)
            for j in range(4):
                score = lax.dot_general(
                    keys[j * step : (j + 1) * step], query, NT, preferred_element_type=jnp.float32
                )
                code = codes[j * step : (j + 1) * step]
                code = jnp.concatenate([code, code], axis=1)
                score = jnp.where((code >= base) & (code < top), score, -1.0)
                best = jnp.maximum(best, jnp.max(score.reshape(step // 8, 8, 256), axis=0))
            found.append(jnp.max(best, axis=0, keepdims=True))
        found = jnp.concatenate(found, axis=1)
        place = lax.broadcasted_iota(jnp.int32, (1, queries), 1) % BLOCK
        found = jnp.where(place >= CAP, over, found)
        found = jnp.broadcast_to(found, (8, queries))
        for k in range(CHIPS):
            line = found if k == 0 else pltpu.roll(found, queries - k * BLOCK, 1)
            row = 8 * (2 * (chip ^ k) + core)
            out_ref[pl.ds(row, 1), :] = line[:1, :128]
            out_ref[pl.ds(row + 1, 1), :] = line[:1, 128:256]


def unpack_kernel(back_ref, slot_ref, best_ref, over_ref):
    me = lax.axis_index("owner")
    chip = me // 2
    core = me % 2
    rows = slot_ref.shape[1]
    best_ref[...] = jnp.zeros_like(best_ref)
    place = lax.broadcasted_iota(jnp.int32, (128, rows), 0)
    row = lax.broadcasted_iota(jnp.int32, (8, 128), 0)
    over_ref[0, 0] = 0
    for k in range(CHIPS):
        home = chip ^ k

        @pl.when(is_home(home))
        def _():
            slot = slot_ref[k : k + 1]
            part = back_ref[pl.ds(pl.multiple_of(8 * (2 * home + core), 8), 8), :]
            total = jnp.zeros((8, rows), jnp.float32)
            for n in range(2):
                value = part[n : n + 1]
                high = value.astype(jnp.bfloat16).astype(jnp.float32)
                middle = (value - high).astype(jnp.bfloat16).astype(jnp.float32)
                low = value - high - middle
                split = jnp.where(row == 0, high, jnp.where(row == 1, middle, jnp.where(row == 2, low, 0.0)))
                hot = (place + 128 * n == slot).astype(jnp.float32).astype(jnp.bfloat16)
                total = total + jnp.dot(
                    split.astype(jnp.bfloat16), hot, preferred_element_type=jnp.float32
                )
            best_ref[...] += jnp.sum(total, axis=0, keepdims=True)
            over_ref[0, 0] = over_ref[0, 0] | (part[1, BLOCK - 1 - 128] > 0.0).astype(jnp.int32)


def meet(embeds, clusters, ranks):
    rows, width = embeds.shape
    vmem = pl.BlockSpec(memory_space=pltpu.VMEM)
    params = pltpu.CompilerParams(vmem_limit_bytes=VMEM_LIMIT)
    packed = pl.pallas_call(
        pack_kernel,
        out_shape=[jax.ShapeDtypeStruct((BLOCK, width), jnp.bfloat16)] * CHIPS
        + [jax.ShapeDtypeStruct((CHIPS, rows), jnp.int32)],
        in_specs=[vmem] * 3,
        out_specs=[vmem] * (CHIPS + 1),
        compiler_params=params,
        name="pack",
    )(embeds, clusters.reshape(1, rows), ranks.reshape(1, rows))
    blocks, slot = list(packed[:CHIPS]), packed[CHIPS]
    for k in (4, 5, 6, 7, 3, 2, 1):
        route = [
            (2 * s + c, 2 * (s ^ k) + c) for s in range(CHIPS) if s ^ k in HOMES for c in range(2)
        ]
        blocks[k] = lax.ppermute(blocks[k], "owner", route)
    swap = [(2 * h + c, 2 * h + 1 - c) for h in HOMES for c in range(2)]
    other = [lax.ppermute(block, "owner", swap) for block in blocks]
    found = pl.pallas_call(
        compare_kernel,
        out_shape=jax.ShapeDtypeStruct((8 * OWNERS, 128), jnp.float32),
        in_specs=[pl.BlockSpec(memory_space=pl.ANY)] * (2 * CHIPS),
        out_specs=vmem,
        scratch_shapes=[
            pltpu.VMEM((2 * CHIPS * BLOCK, width), jnp.bfloat16),
            pltpu.VMEM((2 * CHIPS * BLOCK, 128), jnp.float32),
            pltpu.SemaphoreType.DMA((2 * CHIPS,)),
        ],
        compiler_params=params,
        name="compare",
    )(*blocks, *other)
    back = lax.all_to_all(
        found.reshape(OWNERS, 8, 128), "owner", split_axis=0, concat_axis=0, tiled=True
    )
    best, over = pl.pallas_call(
        unpack_kernel,
        out_shape=[
            jax.ShapeDtypeStruct((1, rows), jnp.float32),
            jax.ShapeDtypeStruct((1, 1), jnp.int32),
        ],
        in_specs=[vmem] * 2,
        out_specs=[vmem, pl.BlockSpec(memory_space=pltpu.SMEM)],
        compiler_params=params,
        name="unpack",
    )(back.reshape(8 * OWNERS, 128), slot)
    return best.reshape(rows), over[0, 0] > 0


def as_sent(array):
    return jax.tree.map(lambda a: a.astype(jnp.bfloat16) if a.dtype == jnp.float32 else a, array)


def from_partner(block, axis, apart):
    count = lax.axis_size(axis)
    route = []
    for low in range(count):
        high = low | 1 << apart
        if high != low and high < count:
            route += [(low, high), (high, low)]
    return lax.ppermute(block, axis, route)


def best_against(best, mine, other):
    mine_unit, mine_cluster, mine_rank = mine
    other_unit, other_cluster, other_rank = other
    query_total = mine_unit.shape[0]
    key_total = other_unit.shape[0]
    query_size = min(512, query_total)
    key_size = min(512, key_total)

    def query_block(query_index, current_best):
        query_start = query_index * query_size
        query_unit = lax.dynamic_slice_in_dim(mine_unit, query_start, query_size, 0)
        query_cluster = lax.dynamic_slice_in_dim(mine_cluster, query_start, query_size, 0)
        query_rank = lax.dynamic_slice_in_dim(mine_rank, query_start, query_size, 0)
        running = lax.dynamic_slice_in_dim(current_best, query_start, query_size, 0)

        def key_block(key_index, running_best):
            key_start = key_index * key_size
            key_unit = lax.dynamic_slice_in_dim(other_unit, key_start, key_size, 0)
            key_cluster = lax.dynamic_slice_in_dim(other_cluster, key_start, key_size, 0)
            key_rank = lax.dynamic_slice_in_dim(other_rank, key_start, key_size, 0)
            allowed = (key_cluster[None, :] == query_cluster[:, None]) & (key_cluster[None, :] >= 0)
            allowed = allowed & (key_rank[None, :] < query_rank[:, None])
            scores = jnp.einsum(
                "qd,kd->qk", query_unit, key_unit, preferred_element_type=jnp.float32
            )
            return jnp.maximum(
                running_best, jnp.max(jnp.where(allowed, scores, jnp.float32(-1.0)), axis=1)
            )

        running = lax.fori_loop(0, key_total // key_size, key_block, running)
        return lax.dynamic_update_slice_in_dim(current_best, running, query_start, 0)

    return lax.fori_loop(0, query_total // query_size, query_block, best)


def route_rows(embeds, clusters, ranks):
    count = lax.axis_size("owner")
    rows, width = embeds.shape
    slots = max(2, 2 * rows // count)
    total = count * slots
    large_cap = total
    values = embeds.astype(jnp.float32)
    unit = (values * lax.rsqrt(jnp.sum(values * values, axis=1, keepdims=True) + 1e-06)).astype(
        jnp.bfloat16
    )
    is_large = clusters >= count
    target = jnp.where(is_large, 8 * (clusters - count) + ranks % 8, clusters)
    positions = jnp.arange(rows, dtype=jnp.int32)
    later = positions[:, None] > positions[None, :]
    earlier = (target[:, None] == target[None, :]) & later
    place = target * slots + jnp.sum(earlier.astype(jnp.int32), axis=1)
    send_unit = jnp.zeros((total, width), jnp.bfloat16).at[place].set(unit)
    send_cluster = jnp.full((total,), -1, jnp.int32).at[place].set(clusters)
    send_rank = jnp.zeros((total,), jnp.int32).at[place].set(ranks)
    got_unit, got_cluster, got_rank = (
        lax.all_to_all(
            send_unit.reshape(count, slots, width), "owner", split_axis=0, concat_axis=0, tiled=True
        ),
        lax.all_to_all(
            send_cluster.reshape(count, slots), "owner", split_axis=0, concat_axis=0, tiled=True
        ),
        lax.all_to_all(
            send_rank.reshape(count, slots), "owner", split_axis=0, concat_axis=0, tiled=True
        ),
    )
    mine = (got_unit.reshape(total, width), got_cluster.reshape(total), got_rank.reshape(total))
    best = jnp.full((total,), -1.0, jnp.float32)
    best = best_against(best, mine, mine)
    large_slot = mine[1] >= count
    large_position = jnp.cumsum(large_slot.astype(jnp.int32)) - 1
    large_place = jnp.where(large_slot, large_position, large_cap)
    large = (
        jnp.zeros((large_cap, width), jnp.bfloat16).at[large_place].set(mine[0], mode="drop"),
        jnp.full((large_cap,), -1, jnp.int32).at[large_place].set(mine[1], mode="drop"),
        jnp.zeros((large_cap,), jnp.int32).at[large_place].set(mine[2], mode="drop"),
    )
    large_best = jnp.full((large_cap,), -1.0, jnp.float32)
    gathered = large
    for level in range(3):
        partner = jax.tree.map(
            lambda part, own: part.astype(own.dtype),
            from_partner(as_sent(gathered), "owner", level),
            gathered,
        )
        large_best = best_against(large_best, large, partner)
        if level < 2:
            gathered = jax.tree.map(
                lambda left, right: jnp.concatenate([left, right], axis=0), gathered, partner
            )
    picked = large_best[jnp.clip(large_position, 0, large_cap - 1)]
    best = jnp.where(large_slot, jnp.maximum(best, picked), best)
    returned = lax.all_to_all(
        best.reshape(count, slots), "owner", split_axis=0, concat_axis=0, tiled=True
    )
    return returned.reshape(total)[place]


def local(embeds, clusters, ranks):
    if lax.axis_size("owner") != OWNERS:
        return route_rows(embeds, clusters, ranks)
    best, over = meet(embeds, clusters, ranks)
    return lax.cond(over, lambda *args: route_rows(*args[:3]), lambda *args: args[3],
                    embeds, clusters, ranks, best)


def solution(mesh):
    return jax.shard_map(
        local,
        mesh=mesh,
        in_specs=(P(("groups", "owner"), None), P(("groups", "owner")), P(("groups", "owner"))),
        out_specs=P(("groups", "owner")),
        check_vma=False,
    )
```

```python
import functools

import jax
import jax.numpy as jnp
from jax import lax
from jax.experimental import pallas as pl
from jax.experimental.pallas import tpu as pltpu
from jax.sharding import PartitionSpec as P

OWNERS = 16
CHIPS = 8
HOMES = (2, 3, 4, 5)
BLOCK = 160
CAP = 156
META = 16
VMEM_LIMIT = 48 * 1024 * 1024
NT = (((1,), (1,)), ((), ()))


def is_home(chip):
    return (chip >= HOMES[0]) & (chip <= HOMES[-1])


def pack_kernel(x_ref, cluster_ref, rank_ref, *outs):
    slot_ref = outs[CHIPS]
    chip = lax.axis_index("owner") // 2
    values = x_ref[...].astype(jnp.float32)
    unit = (values * lax.rsqrt(jnp.sum(values * values, axis=1, keepdims=True) + 1e-06)).astype(
        jnp.bfloat16
    )
    rows, width = unit.shape
    cluster = cluster_ref[...]
    rank = rank_ref[...]
    home = jnp.where(
        cluster < OWNERS // 2,
        3,
        jnp.where(cluster < OWNERS, 4, jnp.where(cluster == OWNERS, 2, 5)),
    )
    number = lax.broadcasted_iota(jnp.int32, (CHIPS, rows), 0)
    member = number == (home ^ chip)
    upper = (
        lax.broadcasted_iota(jnp.int32, (rows, rows), 0)
        < lax.broadcasted_iota(jnp.int32, (rows, rows), 1)
    ).astype(jnp.float32).astype(jnp.bfloat16)
    before = jnp.dot(
        member.astype(jnp.float32).astype(jnp.bfloat16), upper, preferred_element_type=jnp.float32
    )
    slot = jnp.where(member, before.astype(jnp.int32), -1)
    slot_ref[...] = slot
    over = (jnp.max(slot) >= CAP).astype(jnp.float32)
    line = lax.broadcasted_iota(jnp.int32, (META, rows), 0)
    first = META - (BLOCK - CAP)
    meta = jnp.where(
        line == first,
        cluster + 1,
        jnp.where(line == first + 1, rank >> 6, jnp.where(line == first + 2, rank & 63, 0)),
    )
    meta = meta.astype(jnp.float32).astype(jnp.bfloat16)
    for k in range(CHIPS):

        @pl.when(is_home(chip ^ k))
        def _():
            place = lax.broadcasted_iota(jnp.int32, (256, rows), 0)
            hot = ((place == slot[k : k + 1]) & (place < CAP)).astype(jnp.float32)
            hot = hot.astype(jnp.bfloat16)
            block = jnp.dot(hot[:BLOCK], unit, preferred_element_type=jnp.float32)
            outs[k][...] = block.astype(jnp.bfloat16)
            tail = lax.dot_general(meta, hot, NT, preferred_element_type=jnp.float32)
            row = lax.broadcasted_iota(jnp.int32, (META, 256), 0)
            tail = jnp.where(row == META - 1, over, tail)
            tail = jnp.where(row >= first, tail, block[BLOCK - META :, :256])
            outs[k][BLOCK - META :, :256] = tail.astype(jnp.bfloat16)


def fill_codes(keys, codes, first_block, blocks):
    eye = (
        lax.broadcasted_iota(jnp.int32, (BLOCK, 256), 0)
        == lax.broadcasted_iota(jnp.int32, (BLOCK, 256), 1)
    ).astype(jnp.float32).astype(jnp.bfloat16)
    lane = lax.broadcasted_iota(jnp.int32, (1, META), 1)
    first = META - (BLOCK - CAP)
    scale = jnp.where(
        lane == first, 4096.0, jnp.where(lane == first + 1, 64.0, jnp.where(lane == first + 2, 1.0, 0.0))
    )
    over = jnp.zeros((1, 128), jnp.float32)
    for n in range(first_block, first_block + blocks):
        meta = keys[(n + 1) * BLOCK - META : (n + 1) * BLOCK, :256]
        over = jnp.maximum(over, meta[META - 1 :, :128].astype(jnp.float32))
        columns = lax.dot_general(eye, meta, NT, preferred_element_type=jnp.float32)
        code = jnp.sum(columns * scale, axis=1, keepdims=True)
        codes[n * BLOCK : (n + 1) * BLOCK] = jnp.broadcast_to(code, (BLOCK, 128))
    return over


def best_of(keys, codes, key_start, key_count, key_step, query_start, size):
    query = keys[query_start : query_start + size]
    top = jnp.transpose(codes[query_start : query_start + size])[:1]
    base = jnp.floor(top * (1.0 / 4096.0)) * 4096.0
    best = jnp.full((8, size), -1.0, jnp.float32)
    for start in range(key_start, key_start + key_count, key_step):
        score = lax.dot_general(
            keys[start : start + key_step], query, NT, preferred_element_type=jnp.float32
        )
        code = jnp.concatenate([codes[start : start + key_step]] * (size // 128), axis=1)
        score = jnp.where((code >= base) & (code < top), score, -1.0)
        best = jnp.maximum(best, jnp.max(score.reshape(key_step // 8, 8, size), axis=0))
    return best


def fetch(pairs, sems):
    copies = [
        pltpu.make_async_copy(source, target, sems.at[n]) for n, (source, target) in enumerate(pairs)
    ]
    for copy in copies:
        copy.start()
    for copy in copies:
        copy.wait()


def join_kernel(*refs):
    blocks, out_ref, sems = refs[:-2], refs[-2], refs[-1]
    fetch([(ref, out_ref.at[pl.ds(n * BLOCK, BLOCK)]) for n, ref in enumerate(blocks)], sems)


EARLY = (0, 1, 2, 3, 6, 7)
LATE = (4, 5)
EARLY_ROWS = len(EARLY) * BLOCK
LATE_ROWS = len(LATE) * BLOCK
EARLY_QUERIES = 1024
BOTH_QUERIES = 2048
LATE_QUERIES = 384
LATE_START = 2 * EARLY_ROWS


def early_kernel(mine_ref, other_ref, best_ref, over_ref, keys, codes, sems):
    @pl.when(is_home(lax.axis_index("owner") // 2))
    def _():
        fetch(
            [
                (mine_ref, keys.at[pl.ds(0, EARLY_ROWS)]),
                (other_ref, keys.at[pl.ds(EARLY_ROWS, EARLY_ROWS)]),
            ],
            sems,
        )
        over = fill_codes(keys, codes, 0, 2 * len(EARLY))
        over_ref[...] = jnp.broadcast_to(over, over_ref.shape)
        for start in range(0, EARLY_QUERIES, 256):
            best_ref[:, start : start + 256] = best_of(
                keys, codes, 0, 2 * EARLY_ROWS, 640, start, 256
            )


def late_kernel(mine_ref, other_ref, first_ref, second_ref, early_ref, best_ref, late_ref, keys, codes, sems):
    @pl.when(is_home(lax.axis_index("owner") // 2))
    def _():
        fetch(
            [
                (mine_ref, keys.at[pl.ds(0, EARLY_ROWS)]),
                (other_ref, keys.at[pl.ds(EARLY_ROWS, EARLY_ROWS)]),
                (first_ref, keys.at[pl.ds(LATE_START, BLOCK)]),
                (second_ref, keys.at[pl.ds(LATE_START + BLOCK, BLOCK)]),
            ],
            sems,
        )
        fill_codes(keys, codes, 0, 2 * len(EARLY) + len(LATE))
        for start in range(0, BOTH_QUERIES, 256):
            found = best_of(keys, codes, LATE_START, LATE_ROWS, LATE_ROWS, start, 256)
            if start + 256 <= EARLY_ROWS:
                found = jnp.maximum(found, early_ref[:, start : start + 256])
            elif start < EARLY_ROWS:
                lane = lax.broadcasted_iota(jnp.int32, (8, 256), 1)
                known = jnp.where(lane < EARLY_ROWS - start, early_ref[:, start : start + 256], -1.0)
                found = jnp.maximum(found, known)
            best_ref[:, start : start + 256] = found
        late_ref[...] = best_of(
            keys, codes, 0, LATE_START + LATE_ROWS, 448, LATE_START, LATE_QUERIES
        )


def last_kernel(*refs):
    mine, other = refs[: len(LATE)], refs[len(LATE) : 2 * len(LATE)]
    early_ref, late_ref, over_ref, out_ref, keys, codes, sems = refs[2 * len(LATE) :]
    me = lax.axis_index("owner")
    chip = me // 2
    core = me % 2

    @pl.when(is_home(chip))
    def _():
        fetch(
            [
                (ref, keys.at[pl.ds(n * BLOCK, BLOCK)])
                for n, ref in enumerate(mine + other)
            ],
            sems,
        )
        over = fill_codes(keys, codes, 0, 2 * len(LATE))
        over = jnp.max(jnp.maximum(over, over_ref[:1]))
        late = jnp.maximum(
            late_ref[...], best_of(keys, codes, LATE_ROWS, LATE_ROWS, LATE_ROWS, 0, LATE_QUERIES)
        )
        early = early_ref[...]

        def send(found, start, to_chip, to_core):
            line = jnp.max(found, axis=0, keepdims=True)
            line = jnp.broadcast_to(line, (8, line.shape[1]))
            if start:
                line = pltpu.roll(line, line.shape[1] - start, 1)
            row = 8 * (2 * to_chip + to_core)
            out_ref[pl.ds(row, 1), :] = line[:1, :128]
            lane = lax.broadcasted_iota(jnp.int32, (1, 128), 1)
            out_ref[pl.ds(row + 1, 1), :] = jnp.where(lane >= CAP - 128, over, line[:1, 128:256])

        early = jnp.max(early, axis=0, keepdims=True)
        late = jnp.max(late, axis=0, keepdims=True)
        for n, k in enumerate(EARLY):
            send(early, n * BLOCK, chip ^ k, core)
            send(early, EARLY_ROWS + n * BLOCK, chip ^ k, 1 - core)
        for n, k in enumerate(LATE):
            send(late, n * BLOCK, chip ^ k, core)


def unpack_kernel(back_ref, slot_ref, best_ref, over_ref):
    me = lax.axis_index("owner")
    chip = me // 2
    core = me % 2
    rows = slot_ref.shape[1]
    best_ref[...] = jnp.zeros_like(best_ref)
    place = lax.broadcasted_iota(jnp.int32, (128, rows), 0)
    row = lax.broadcasted_iota(jnp.int32, (8, 128), 0)
    over_ref[0, 0] = 0
    for k in range(CHIPS):
        home = chip ^ k

        @pl.when(is_home(home))
        def _():
            slot = slot_ref[k : k + 1]
            part = back_ref[pl.ds(pl.multiple_of(8 * (2 * home + core), 8), 8), :]
            if k in EARLY:
                second = back_ref[pl.ds(pl.multiple_of(8 * (2 * home + 1 - core), 8), 8), :]
                part = jnp.maximum(part, second)
            total = jnp.zeros((8, rows), jnp.float32)
            for n in range(2):
                value = part[n : n + 1]
                high = value.astype(jnp.bfloat16).astype(jnp.float32)
                middle = (value - high).astype(jnp.bfloat16).astype(jnp.float32)
                low = value - high - middle
                split = jnp.where(row == 0, high, jnp.where(row == 1, middle, jnp.where(row == 2, low, 0.0)))
                hot = (place + 128 * n == slot).astype(jnp.float32).astype(jnp.bfloat16)
                total = total + jnp.dot(
                    split.astype(jnp.bfloat16), hot, preferred_element_type=jnp.float32
                )
            best_ref[...] += jnp.sum(total, axis=0, keepdims=True)
            over_ref[0, 0] = over_ref[0, 0] | (part[1, BLOCK - 1 - 128] > 0.0).astype(jnp.int32)


def meet(embeds, clusters, ranks):
    rows, width = embeds.shape
    vmem = pl.BlockSpec(memory_space=pltpu.VMEM)
    params = pltpu.CompilerParams(vmem_limit_bytes=VMEM_LIMIT)
    packed = pl.pallas_call(
        pack_kernel,
        out_shape=[jax.ShapeDtypeStruct((BLOCK, width), jnp.bfloat16)] * CHIPS
        + [jax.ShapeDtypeStruct((CHIPS, rows), jnp.int32)],
        in_specs=[vmem] * 3,
        out_specs=[vmem] * (CHIPS + 1),
        compiler_params=params,
        name="pack",
    )(embeds, clusters.reshape(1, rows), ranks.reshape(1, rows))
    blocks, slot = list(packed[:CHIPS]), packed[CHIPS]
    for k in (2, 3, 6, 7, 1, 4, 5):
        route = [
            (2 * s + c, 2 * (s ^ k) + c) for s in range(CHIPS) if s ^ k in HOMES for c in range(2)
        ]
        blocks[k] = lax.ppermute(blocks[k], "owner", route)
    swap = [(2 * h + c, 2 * h + 1 - c) for h in HOMES for c in range(2)]
    anywhere = pl.BlockSpec(memory_space=pl.ANY)

    def keys_scratch(total, copies):
        return [
            pltpu.VMEM((total, width), jnp.bfloat16),
            pltpu.VMEM((total, 128), jnp.float32),
            pltpu.SemaphoreType.DMA((copies,)),
        ]

    def cost(pairs):
        return pl.CostEstimate(
            flops=8 * pairs * width, bytes_accessed=2 * 2 * EARLY_ROWS * width, transcendentals=0
        )

    mine = pl.pallas_call(
        join_kernel,
        out_shape=jax.ShapeDtypeStruct((EARLY_ROWS, width), jnp.bfloat16),
        in_specs=[anywhere] * len(EARLY),
        out_specs=anywhere,
        scratch_shapes=[pltpu.SemaphoreType.DMA((len(EARLY),))],
        name="join",
    )(*[blocks[k] for k in EARLY])
    other = lax.ppermute(mine, "owner", swap)
    late_mine = [blocks[k] for k in LATE]
    late_other = [lax.ppermute(block, "owner", swap) for block in late_mine]
    early, over = pl.pallas_call(
        early_kernel,
        out_shape=[
            jax.ShapeDtypeStruct((8, EARLY_QUERIES), jnp.float32),
            jax.ShapeDtypeStruct((8, 128), jnp.float32),
        ],
        in_specs=[anywhere] * 2,
        out_specs=[vmem] * 2,
        scratch_shapes=keys_scratch(2 * EARLY_ROWS, 2),
        compiler_params=params,
        cost_estimate=cost(EARLY_QUERIES * 2 * EARLY_ROWS),
        name="early",
    )(mine, other)
    early, late = pl.pallas_call(
        late_kernel,
        out_shape=[
            jax.ShapeDtypeStruct((8, BOTH_QUERIES), jnp.float32),
            jax.ShapeDtypeStruct((8, LATE_QUERIES), jnp.float32),
        ],
        in_specs=[anywhere] * 4 + [vmem],
        out_specs=[vmem] * 2,
        scratch_shapes=keys_scratch(max(BOTH_QUERIES, LATE_START + LATE_QUERIES), 4),
        compiler_params=params,
        cost_estimate=cost(BOTH_QUERIES * LATE_ROWS + LATE_QUERIES * 2 * EARLY_ROWS),
        name="late",
    )(mine, other, *late_mine, early)
    found = pl.pallas_call(
        last_kernel,
        out_shape=jax.ShapeDtypeStruct((8 * OWNERS, 128), jnp.float32),
        in_specs=[anywhere] * (2 * len(LATE)) + [vmem] * 3,
        out_specs=vmem,
        scratch_shapes=keys_scratch(2 * LATE_ROWS, 2 * len(LATE)),
        compiler_params=params,
        name="last",
    )(*late_mine, *late_other, early, late, over)
    back = lax.all_to_all(
        found.reshape(OWNERS, 8, 128), "owner", split_axis=0, concat_axis=0, tiled=True
    )
    best, over = pl.pallas_call(
        unpack_kernel,
        out_shape=[
            jax.ShapeDtypeStruct((1, rows), jnp.float32),
            jax.ShapeDtypeStruct((1, 1), jnp.int32),
        ],
        in_specs=[vmem] * 2,
        out_specs=[vmem, pl.BlockSpec(memory_space=pltpu.SMEM)],
        compiler_params=params,
        name="unpack",
    )(back.reshape(8 * OWNERS, 128), slot)
    return best.reshape(rows), over[0, 0] > 0


def as_sent(array):
    return jax.tree.map(lambda a: a.astype(jnp.bfloat16) if a.dtype == jnp.float32 else a, array)


def from_partner(block, axis, apart):
    count = lax.axis_size(axis)
    route = []
    for low in range(count):
        high = low | 1 << apart
        if high != low and high < count:
            route += [(low, high), (high, low)]
    return lax.ppermute(block, axis, route)


def best_against(best, mine, other):
    mine_unit, mine_cluster, mine_rank = mine
    other_unit, other_cluster, other_rank = other
    query_total = mine_unit.shape[0]
    key_total = other_unit.shape[0]
    query_size = min(512, query_total)
    key_size = min(512, key_total)

    def query_block(query_index, current_best):
        query_start = query_index * query_size
        query_unit = lax.dynamic_slice_in_dim(mine_unit, query_start, query_size, 0)
        query_cluster = lax.dynamic_slice_in_dim(mine_cluster, query_start, query_size, 0)
        query_rank = lax.dynamic_slice_in_dim(mine_rank, query_start, query_size, 0)
        running = lax.dynamic_slice_in_dim(current_best, query_start, query_size, 0)

        def key_block(key_index, running_best):
            key_start = key_index * key_size
            key_unit = lax.dynamic_slice_in_dim(other_unit, key_start, key_size, 0)
            key_cluster = lax.dynamic_slice_in_dim(other_cluster, key_start, key_size, 0)
            key_rank = lax.dynamic_slice_in_dim(other_rank, key_start, key_size, 0)
            allowed = (key_cluster[None, :] == query_cluster[:, None]) & (key_cluster[None, :] >= 0)
            allowed = allowed & (key_rank[None, :] < query_rank[:, None])
            scores = jnp.einsum(
                "qd,kd->qk", query_unit, key_unit, preferred_element_type=jnp.float32
            )
            return jnp.maximum(
                running_best, jnp.max(jnp.where(allowed, scores, jnp.float32(-1.0)), axis=1)
            )

        running = lax.fori_loop(0, key_total // key_size, key_block, running)
        return lax.dynamic_update_slice_in_dim(current_best, running, query_start, 0)

    return lax.fori_loop(0, query_total // query_size, query_block, best)


def route_rows(embeds, clusters, ranks):
    count = lax.axis_size("owner")
    rows, width = embeds.shape
    slots = max(2, 2 * rows // count)
    total = count * slots
    large_cap = total
    values = embeds.astype(jnp.float32)
    unit = (values * lax.rsqrt(jnp.sum(values * values, axis=1, keepdims=True) + 1e-06)).astype(
        jnp.bfloat16
    )
    is_large = clusters >= count
    target = jnp.where(is_large, 8 * (clusters - count) + ranks % 8, clusters)
    positions = jnp.arange(rows, dtype=jnp.int32)
    later = positions[:, None] > positions[None, :]
    earlier = (target[:, None] == target[None, :]) & later
    place = target * slots + jnp.sum(earlier.astype(jnp.int32), axis=1)
    send_unit = jnp.zeros((total, width), jnp.bfloat16).at[place].set(unit)
    send_cluster = jnp.full((total,), -1, jnp.int32).at[place].set(clusters)
    send_rank = jnp.zeros((total,), jnp.int32).at[place].set(ranks)
    got_unit, got_cluster, got_rank = (
        lax.all_to_all(
            send_unit.reshape(count, slots, width), "owner", split_axis=0, concat_axis=0, tiled=True
        ),
        lax.all_to_all(
            send_cluster.reshape(count, slots), "owner", split_axis=0, concat_axis=0, tiled=True
        ),
        lax.all_to_all(
            send_rank.reshape(count, slots), "owner", split_axis=0, concat_axis=0, tiled=True
        ),
    )
    mine = (got_unit.reshape(total, width), got_cluster.reshape(total), got_rank.reshape(total))
    best = jnp.full((total,), -1.0, jnp.float32)
    best = best_against(best, mine, mine)
    large_slot = mine[1] >= count
    large_position = jnp.cumsum(large_slot.astype(jnp.int32)) - 1
    large_place = jnp.where(large_slot, large_position, large_cap)
    large = (
        jnp.zeros((large_cap, width), jnp.bfloat16).at[large_place].set(mine[0], mode="drop"),
        jnp.full((large_cap,), -1, jnp.int32).at[large_place].set(mine[1], mode="drop"),
        jnp.zeros((large_cap,), jnp.int32).at[large_place].set(mine[2], mode="drop"),
    )
    large_best = jnp.full((large_cap,), -1.0, jnp.float32)
    gathered = large
    for level in range(3):
        partner = jax.tree.map(
            lambda part, own: part.astype(own.dtype),
            from_partner(as_sent(gathered), "owner", level),
            gathered,
        )
        large_best = best_against(large_best, large, partner)
        if level < 2:
            gathered = jax.tree.map(
                lambda left, right: jnp.concatenate([left, right], axis=0), gathered, partner
            )
    picked = large_best[jnp.clip(large_position, 0, large_cap - 1)]
    best = jnp.where(large_slot, jnp.maximum(best, picked), best)
    returned = lax.all_to_all(
        best.reshape(count, slots), "owner", split_axis=0, concat_axis=0, tiled=True
    )
    return returned.reshape(total)[place]


def local(embeds, clusters, ranks):
    if lax.axis_size("owner") != OWNERS:
        return route_rows(embeds, clusters, ranks)
    best, over = meet(embeds, clusters, ranks)
    return lax.cond(over, lambda *args: route_rows(*args[:3]), lambda *args: args[3],
                    embeds, clusters, ranks, best)


def solution(mesh):
    return jax.shard_map(
        local,
        mesh=mesh,
        in_specs=(P(("groups", "owner"), None), P(("groups", "owner")), P(("groups", "owner"))),
        out_specs=P(("groups", "owner")),
        check_vma=False,
    )
```

```python
import functools

import jax
import jax.numpy as jnp
from jax import lax
from jax.experimental import pallas as pl
from jax.experimental.pallas import tpu as pltpu
from jax.sharding import PartitionSpec as P

OWNERS = 16
CHIPS = 8
HOMES = (2, 3, 4, 5)
HOME_ROUNDS = (0, 1, 6, 7)
OUTER_ROUNDS = (2, 3, 4, 5)
BLOCK = 160
CAP = 156
META = 16
HELD = CHIPS * BLOCK
VMEM_LIMIT = 48 * 1024 * 1024
NT = (((1,), (1,)), ((), ()))


def is_home(chip):
    return (chip >= HOMES[0]) & (chip <= HOMES[-1])


def pack_kernel(x_ref, cluster_ref, rank_ref, *outs):
    slot_ref = outs[len(HOMES)]
    chip = lax.axis_index("owner") // 2
    values = x_ref[...].astype(jnp.float32)
    unit = (values * lax.rsqrt(jnp.sum(values * values, axis=1, keepdims=True) + 1e-06)).astype(
        jnp.bfloat16
    )
    rows, width = unit.shape
    cluster = cluster_ref[...]
    rank = rank_ref[...]
    home = jnp.where(
        cluster < OWNERS // 2,
        3,
        jnp.where(cluster < OWNERS, 4, jnp.where(cluster == OWNERS, 2, 5)),
    )
    number = lax.broadcasted_iota(jnp.int32, (8, rows), 0)
    member = number + HOMES[0] == home
    upper = (
        lax.broadcasted_iota(jnp.int32, (rows, rows), 0)
        < lax.broadcasted_iota(jnp.int32, (rows, rows), 1)
    ).astype(jnp.float32).astype(jnp.bfloat16)
    before = jnp.dot(
        member.astype(jnp.float32).astype(jnp.bfloat16), upper, preferred_element_type=jnp.float32
    )
    slot = jnp.where(member, before.astype(jnp.int32), -1)
    slot_ref[...] = slot
    over = (jnp.max(slot) >= CAP).astype(jnp.float32)
    line = lax.broadcasted_iota(jnp.int32, (META, rows), 0)
    first = META - (BLOCK - CAP)
    meta = jnp.where(
        line == first,
        cluster + 1,
        jnp.where(line == first + 1, rank >> 6, jnp.where(line == first + 2, rank & 63, 0)),
    )
    meta = meta.astype(jnp.float32).astype(jnp.bfloat16)
    place = lax.broadcasted_iota(jnp.int32, (256, rows), 0)
    for n in range(len(HOMES)):
        k = jnp.where(is_home(chip), HOME_ROUNDS[n], OUTER_ROUNDS[n])
        mine = slot_ref[pl.ds((chip ^ k) - HOMES[0], 1), :]
        hot = ((place == mine) & (place < CAP)).astype(jnp.float32).astype(jnp.bfloat16)
        block = jnp.dot(hot[:BLOCK], unit, preferred_element_type=jnp.float32)
        outs[n][...] = block.astype(jnp.bfloat16)
        tail = lax.dot_general(meta, hot, NT, preferred_element_type=jnp.float32)
        row = lax.broadcasted_iota(jnp.int32, (META, 256), 0)
        tail = jnp.where(row == META - 1, over, tail)
        tail = jnp.where(row >= first, tail, block[BLOCK - META :, :256])
        outs[n][BLOCK - META :, :256] = tail.astype(jnp.bfloat16)


def fill_codes(keys, codes):
    eye = (
        lax.broadcasted_iota(jnp.int32, (BLOCK, 256), 0)
        == lax.broadcasted_iota(jnp.int32, (BLOCK, 256), 1)
    ).astype(jnp.float32).astype(jnp.bfloat16)
    lane = lax.broadcasted_iota(jnp.int32, (1, META), 1)
    first = META - (BLOCK - CAP)
    scale = jnp.where(
        lane == first, 4096.0, jnp.where(lane == first + 1, 64.0, jnp.where(lane == first + 2, 1.0, 0.0))
    )
    over = jnp.zeros((1, 128), jnp.float32)
    for n in range(CHIPS):
        meta = keys[(n + 1) * BLOCK - META : (n + 1) * BLOCK, :256]
        over = jnp.maximum(over, meta[META - 1 :, :128].astype(jnp.float32))
        columns = lax.dot_general(eye, meta, NT, preferred_element_type=jnp.float32)
        code = jnp.sum(columns * scale, axis=1, keepdims=True)
        codes[n * BLOCK : (n + 1) * BLOCK] = jnp.broadcast_to(code, (BLOCK, 128))
    return over


def best_of(keys, codes, query, top):
    size = query.shape[0]
    step = HELD // 2
    base = jnp.floor(top * (1.0 / 4096.0)) * 4096.0
    best = jnp.full((8, size), -1.0, jnp.float32)
    for start in range(0, HELD, step):
        score = lax.dot_general(
            keys[start : start + step], query, NT, preferred_element_type=jnp.float32
        )
        code = jnp.concatenate([codes[start : start + step]] * (size // 128), axis=1)
        score = jnp.where((code >= base) & (code < top), score, -1.0)
        best = jnp.maximum(best, jnp.max(score.reshape(step // 8, 8, size), axis=0))
    return best


def join_kernel(*refs):
    blocks, out_ref, sems = refs[:-2], refs[-2], refs[-1]
    copies = [
        pltpu.make_async_copy(ref, out_ref.at[pl.ds(n * BLOCK, BLOCK)], sems.at[n])
        for n, ref in enumerate(blocks)
    ]
    for copy in copies:
        copy.start()
    for copy in copies:
        copy.wait()


def own_kernel(mine_ref, best_ref, top_ref, over_ref, codes):
    @pl.when(is_home(lax.axis_index("owner") // 2))
    def _():
        over_ref[...] = jnp.broadcast_to(fill_codes(mine_ref, codes), over_ref.shape)
        for at in range(0, HELD, 256):
            top = jnp.transpose(codes[at : at + 256])[:8]
            top_ref[:, at : at + 256] = top
            best_ref[:, at : at + 256] = best_of(
                mine_ref, codes, mine_ref[at : at + 256], top[:1]
            )


def other_kernel(mine_ref, other_ref, best_ref, top_ref, over_ref, out_ref, codes):
    me = lax.axis_index("owner")
    chip = me // 2
    core = me % 2

    @pl.when(is_home(chip))
    def _():
        over = jnp.max(jnp.maximum(fill_codes(other_ref, codes), over_ref[:1]))
        found = [
            jnp.maximum(
                best_ref[:, at : at + 256],
                best_of(other_ref, codes, mine_ref[at : at + 256], top_ref[:1, at : at + 256]),
            )
            for at in range(0, HELD, 256)
        ]
        found = jnp.max(jnp.concatenate(found, axis=1), axis=0, keepdims=True)
        found = jnp.broadcast_to(found, (8, HELD))
        lane = lax.broadcasted_iota(jnp.int32, (1, 128), 1)
        for k in range(CHIPS):
            start = k * BLOCK
            base = min(start // 128 * 128, HELD - 256)
            size = min(384, HELD - base)
            part = found[:, base : base + size]
            if start > base:
                part = pltpu.roll(part, size - (start - base), 1)
            row = 8 * (2 * (chip ^ k) + core)
            out_ref[pl.ds(row, 1), :] = part[:1, :128]
            out_ref[pl.ds(row + 1, 1), :] = jnp.where(lane >= CAP - 128, over, part[:1, 128:256])


def unpack_kernel(back_ref, slot_ref, best_ref, over_ref):
    core = lax.axis_index("owner") % 2
    rows = slot_ref.shape[1]
    place = lax.broadcasted_iota(jnp.int32, (128, rows), 0)
    row = lax.broadcasted_iota(jnp.int32, (8, 128), 0)
    total = jnp.zeros((8, rows), jnp.float32)
    over = jnp.zeros((8, 128), jnp.float32)
    for n, home in enumerate(HOMES):
        part = back_ref[pl.ds(pl.multiple_of(8 * (2 * home + core), 8), 8), :]
        over = jnp.maximum(over, part)
        for half in range(2):
            value = part[half : half + 1]
            high = value.astype(jnp.bfloat16).astype(jnp.float32)
            middle = (value - high).astype(jnp.bfloat16).astype(jnp.float32)
            low = value - high - middle
            split = jnp.where(row == 0, high, jnp.where(row == 1, middle, jnp.where(row == 2, low, 0.0)))
            hot = (place + 128 * half == slot_ref[n : n + 1]) & (place + 128 * half < BLOCK)
            total = total + jnp.dot(
                split.astype(jnp.bfloat16),
                hot.astype(jnp.float32).astype(jnp.bfloat16),
                preferred_element_type=jnp.float32,
            )
    best_ref[...] = jnp.sum(total, axis=0, keepdims=True)
    over_ref[0, 0] = (over[1, BLOCK - 1 - 128] > 0.0).astype(jnp.int32)


def meet(embeds, clusters, ranks):
    rows, width = embeds.shape
    vmem = pl.BlockSpec(memory_space=pltpu.VMEM)
    params = pltpu.CompilerParams(vmem_limit_bytes=VMEM_LIMIT)
    *sent, slot = pl.pallas_call(
        pack_kernel,
        out_shape=[jax.ShapeDtypeStruct((BLOCK, width), jnp.bfloat16)] * len(HOMES)
        + [jax.ShapeDtypeStruct((8, rows), jnp.int32)],
        in_specs=[vmem] * 3,
        out_specs=[vmem] * (len(HOMES) + 1),
        compiler_params=params,
        name="pack",
    )(embeds, clusters.reshape(1, rows), ranks.reshape(1, rows))
    blocks = {0: sent[0]}
    for k in range(1, CHIPS):
        route = [
            (2 * s + c, 2 * (s ^ k) + c) for s in range(CHIPS) if s ^ k in HOMES for c in range(2)
        ]
        rounds = HOME_ROUNDS if k in HOME_ROUNDS else OUTER_ROUNDS
        blocks[k] = lax.ppermute(sent[rounds.index(k)], "owner", route)
    swap = [(2 * h + c, 2 * h + 1 - c) for h in HOMES for c in range(2)]
    anywhere = pl.BlockSpec(memory_space=pl.ANY)

    line = jax.ShapeDtypeStruct((8, HELD), jnp.float32)
    codes = [pltpu.VMEM((HELD, 128), jnp.float32)]
    cost = pl.CostEstimate(
        flops=2 * HELD * HELD * width, bytes_accessed=2 * HELD * width, transcendentals=0
    )
    mine = pl.pallas_call(
        join_kernel,
        out_shape=jax.ShapeDtypeStruct((HELD, width), jnp.bfloat16),
        in_specs=[anywhere] * CHIPS,
        out_specs=vmem,
        scratch_shapes=[pltpu.SemaphoreType.DMA((CHIPS,))],
        compiler_params=params,
        name="join",
    )(*[blocks[k] for k in range(CHIPS)])
    other = lax.ppermute(mine, "owner", swap)
    best, top, over = pl.pallas_call(
        own_kernel,
        out_shape=[line, line, jax.ShapeDtypeStruct((8, 128), jnp.float32)],
        in_specs=[vmem],
        out_specs=[vmem] * 3,
        scratch_shapes=codes,
        compiler_params=params,
        cost_estimate=cost,
        name="own",
    )(mine)
    found = pl.pallas_call(
        other_kernel,
        out_shape=jax.ShapeDtypeStruct((8 * OWNERS, 128), jnp.float32),
        in_specs=[vmem] * 5,
        out_specs=vmem,
        scratch_shapes=codes,
        compiler_params=params,
        cost_estimate=cost,
        name="other",
    )(mine, other, best, top, over)
    back = lax.all_to_all(
        found.reshape(OWNERS, 8, 128), "owner", split_axis=0, concat_axis=0, tiled=True
    )
    best, over = pl.pallas_call(
        unpack_kernel,
        out_shape=[
            jax.ShapeDtypeStruct((1, rows), jnp.float32),
            jax.ShapeDtypeStruct((1, 1), jnp.int32),
        ],
        in_specs=[vmem] * 2,
        out_specs=[vmem, pl.BlockSpec(memory_space=pltpu.SMEM)],
        compiler_params=params,
        name="unpack",
    )(back.reshape(8 * OWNERS, 128), slot)
    return best.reshape(rows), over[0, 0] > 0


def as_sent(array):
    return jax.tree.map(lambda a: a.astype(jnp.bfloat16) if a.dtype == jnp.float32 else a, array)


def from_partner(block, axis, apart):
    count = lax.axis_size(axis)
    route = []
    for low in range(count):
        high = low | 1 << apart
        if high != low and high < count:
            route += [(low, high), (high, low)]
    return lax.ppermute(block, axis, route)


def best_against(best, mine, other):
    mine_unit, mine_cluster, mine_rank = mine
    other_unit, other_cluster, other_rank = other
    query_total = mine_unit.shape[0]
    key_total = other_unit.shape[0]
    query_size = min(512, query_total)
    key_size = min(512, key_total)

    def query_block(query_index, current_best):
        query_start = query_index * query_size
        query_unit = lax.dynamic_slice_in_dim(mine_unit, query_start, query_size, 0)
        query_cluster = lax.dynamic_slice_in_dim(mine_cluster, query_start, query_size, 0)
        query_rank = lax.dynamic_slice_in_dim(mine_rank, query_start, query_size, 0)
        running = lax.dynamic_slice_in_dim(current_best, query_start, query_size, 0)

        def key_block(key_index, running_best):
            key_start = key_index * key_size
            key_unit = lax.dynamic_slice_in_dim(other_unit, key_start, key_size, 0)
            key_cluster = lax.dynamic_slice_in_dim(other_cluster, key_start, key_size, 0)
            key_rank = lax.dynamic_slice_in_dim(other_rank, key_start, key_size, 0)
            allowed = (key_cluster[None, :] == query_cluster[:, None]) & (key_cluster[None, :] >= 0)
            allowed = allowed & (key_rank[None, :] < query_rank[:, None])
            scores = jnp.einsum(
                "qd,kd->qk", query_unit, key_unit, preferred_element_type=jnp.float32
            )
            return jnp.maximum(
                running_best, jnp.max(jnp.where(allowed, scores, jnp.float32(-1.0)), axis=1)
            )

        running = lax.fori_loop(0, key_total // key_size, key_block, running)
        return lax.dynamic_update_slice_in_dim(current_best, running, query_start, 0)

    return lax.fori_loop(0, query_total // query_size, query_block, best)


def route_rows(embeds, clusters, ranks):
    count = lax.axis_size("owner")
    rows, width = embeds.shape
    slots = max(2, 2 * rows // count)
    total = count * slots
    large_cap = total
    values = embeds.astype(jnp.float32)
    unit = (values * lax.rsqrt(jnp.sum(values * values, axis=1, keepdims=True) + 1e-06)).astype(
        jnp.bfloat16
    )
    is_large = clusters >= count
    target = jnp.where(is_large, 8 * (clusters - count) + ranks % 8, clusters)
    positions = jnp.arange(rows, dtype=jnp.int32)
    later = positions[:, None] > positions[None, :]
    earlier = (target[:, None] == target[None, :]) & later
    place = target * slots + jnp.sum(earlier.astype(jnp.int32), axis=1)
    send_unit = jnp.zeros((total, width), jnp.bfloat16).at[place].set(unit)
    send_cluster = jnp.full((total,), -1, jnp.int32).at[place].set(clusters)
    send_rank = jnp.zeros((total,), jnp.int32).at[place].set(ranks)
    got_unit, got_cluster, got_rank = (
        lax.all_to_all(
            send_unit.reshape(count, slots, width), "owner", split_axis=0, concat_axis=0, tiled=True
        ),
        lax.all_to_all(
            send_cluster.reshape(count, slots), "owner", split_axis=0, concat_axis=0, tiled=True
        ),
        lax.all_to_all(
            send_rank.reshape(count, slots), "owner", split_axis=0, concat_axis=0, tiled=True
        ),
    )
    mine = (got_unit.reshape(total, width), got_cluster.reshape(total), got_rank.reshape(total))
    best = jnp.full((total,), -1.0, jnp.float32)
    best = best_against(best, mine, mine)
    large_slot = mine[1] >= count
    large_position = jnp.cumsum(large_slot.astype(jnp.int32)) - 1
    large_place = jnp.where(large_slot, large_position, large_cap)
    large = (
        jnp.zeros((large_cap, width), jnp.bfloat16).at[large_place].set(mine[0], mode="drop"),
        jnp.full((large_cap,), -1, jnp.int32).at[large_place].set(mine[1], mode="drop"),
        jnp.zeros((large_cap,), jnp.int32).at[large_place].set(mine[2], mode="drop"),
    )
    large_best = jnp.full((large_cap,), -1.0, jnp.float32)
    gathered = large
    for level in range(3):
        partner = jax.tree.map(
            lambda part, own: part.astype(own.dtype),
            from_partner(as_sent(gathered), "owner", level),
            gathered,
        )
        large_best = best_against(large_best, large, partner)
        if level < 2:
            gathered = jax.tree.map(
                lambda left, right: jnp.concatenate([left, right], axis=0), gathered, partner
            )
    picked = large_best[jnp.clip(large_position, 0, large_cap - 1)]
    best = jnp.where(large_slot, jnp.maximum(best, picked), best)
    returned = lax.all_to_all(
        best.reshape(count, slots), "owner", split_axis=0, concat_axis=0, tiled=True
    )
    return returned.reshape(total)[place]


def local(embeds, clusters, ranks):
    if lax.axis_size("owner") != OWNERS:
        return route_rows(embeds, clusters, ranks)
    best, over = meet(embeds, clusters, ranks)
    return lax.cond(over, lambda *args: route_rows(*args[:3]), lambda *args: args[3],
                    embeds, clusters, ranks, best)


def solution(mesh):
    return jax.shard_map(
        local,
        mesh=mesh,
        in_specs=(P(("groups", "owner"), None), P(("groups", "owner")), P(("groups", "owner"))),
        out_specs=P(("groups", "owner")),
        check_vma=False,
    )
```

```python
import functools

import jax
import jax.numpy as jnp
from jax import lax
from jax.experimental import pallas as pl
from jax.experimental.pallas import tpu as pltpu
from jax.sharding import PartitionSpec as P

OWNERS = 16
CHIPS = 8
HOMES = (2, 3, 4, 5)
HOME_ROUNDS = (0, 1, 6, 7)
OUTER_ROUNDS = (2, 3, 4, 5)
ORDER = (0,1,3,6,7,4,5,2)
BLOCK = 160
CAP = 156
META = 16
HELD = CHIPS * BLOCK
VMEM_LIMIT = 48 * 1024 * 1024
NT = (((1,), (1,)), ((), ()))


def is_home(chip):
    return (chip >= HOMES[0]) & (chip <= HOMES[-1])


def pack_kernel(x_ref, cluster_ref, rank_ref, *outs):
    slot_ref = outs[len(HOMES)]
    chip = lax.axis_index("owner") // 2
    values = x_ref[...].astype(jnp.float32)
    unit = (values * lax.rsqrt(jnp.sum(values * values, axis=1, keepdims=True) + 1e-06)).astype(
        jnp.bfloat16
    )
    rows, width = unit.shape
    cluster = cluster_ref[...]
    rank = rank_ref[...]
    home = jnp.where(
        cluster < OWNERS // 2,
        3,
        jnp.where(cluster < OWNERS, 4, jnp.where(cluster == OWNERS, 2, 5)),
    )
    number = lax.broadcasted_iota(jnp.int32, (8, rows), 0)
    member = number + HOMES[0] == home
    upper = (
        lax.broadcasted_iota(jnp.int32, (rows, rows), 0)
        < lax.broadcasted_iota(jnp.int32, (rows, rows), 1)
    ).astype(jnp.float32).astype(jnp.bfloat16)
    before = jnp.dot(
        member.astype(jnp.float32).astype(jnp.bfloat16), upper, preferred_element_type=jnp.float32
    )
    slot = jnp.where(member, before.astype(jnp.int32), -1)
    slot_ref[...] = slot
    over = (jnp.max(slot) >= CAP).astype(jnp.float32)
    line = lax.broadcasted_iota(jnp.int32, (META, rows), 0)
    first = META - (BLOCK - CAP)
    meta = jnp.where(
        line == first,
        cluster + 1,
        jnp.where(line == first + 1, rank >> 6, jnp.where(line == first + 2, rank & 63, 0)),
    )
    meta = meta.astype(jnp.float32).astype(jnp.bfloat16)
    place = lax.broadcasted_iota(jnp.int32, (256, rows), 0)
    for n in range(len(HOMES)):
        k = jnp.where(is_home(chip), HOME_ROUNDS[n], OUTER_ROUNDS[n])
        mine = slot_ref[pl.ds((chip ^ k) - HOMES[0], 1), :]
        hot = ((place == mine) & (place < CAP)).astype(jnp.float32).astype(jnp.bfloat16)
        block = jnp.dot(hot[:BLOCK], unit, preferred_element_type=jnp.float32)
        outs[n][...] = block.astype(jnp.bfloat16)
        tail = lax.dot_general(meta, hot, NT, preferred_element_type=jnp.float32)
        row = lax.broadcasted_iota(jnp.int32, (META, 256), 0)
        tail = jnp.where(row == META - 1, over, tail)
        tail = jnp.where(row >= first, tail, block[BLOCK - META :, :256])
        outs[n][BLOCK - META :, :256] = tail.astype(jnp.bfloat16)


def fill_codes(keys, codes):
    eye = (
        lax.broadcasted_iota(jnp.int32, (BLOCK, 256), 0)
        == lax.broadcasted_iota(jnp.int32, (BLOCK, 256), 1)
    ).astype(jnp.float32).astype(jnp.bfloat16)
    lane = lax.broadcasted_iota(jnp.int32, (1, META), 1)
    first = META - (BLOCK - CAP)
    scale = jnp.where(
        lane == first, 4096.0, jnp.where(lane == first + 1, 64.0, jnp.where(lane == first + 2, 1.0, 0.0))
    )
    over = jnp.zeros((1, 128), jnp.float32)
    for n in range(CHIPS):
        meta = keys[(n + 1) * BLOCK - META : (n + 1) * BLOCK, :256]
        over = jnp.maximum(over, meta[META - 1 :, :128].astype(jnp.float32))
        columns = lax.dot_general(eye, meta, NT, preferred_element_type=jnp.float32)
        code = jnp.sum(columns * scale, axis=1, keepdims=True)
        codes[n * BLOCK : (n + 1) * BLOCK] = jnp.broadcast_to(code, (BLOCK, 128))
    return over


def best_of(keys, codes, query, top):
    size = query.shape[0]
    step = HELD // 2
    base = jnp.floor(top * (1.0 / 4096.0)) * 4096.0
    best = jnp.full((8, size), -1.0, jnp.float32)
    for start in range(0, HELD, step):
        score = lax.dot_general(
            keys[start : start + step], query, NT, preferred_element_type=jnp.float32
        )
        code = jnp.concatenate([codes[start : start + step]] * (size // 128), axis=1)
        score = jnp.where((code >= base) & (code < top), score, -1.0)
        best = jnp.maximum(best, jnp.max(score.reshape(step // 8, 8, size), axis=0))
    return best


def join_kernel(*refs):
    blocks, out_ref = refs[:-1], refs[-1]
    for n, ref in enumerate(blocks):
        out_ref[n * BLOCK : (n + 1) * BLOCK] = ref[...]


def own_kernel(mine_ref, best_ref, top_ref, over_ref, codes):
    @pl.when(is_home(lax.axis_index("owner") // 2))
    def _():
        over_ref[...] = jnp.broadcast_to(fill_codes(mine_ref, codes), over_ref.shape)
        for at in range(0, HELD, 256):
            top = jnp.transpose(codes[at : at + 256])[:8]
            top_ref[:, at : at + 256] = top
            best_ref[:, at : at + 256] = best_of(
                mine_ref, codes, mine_ref[at : at + 256], top[:1]
            )


def other_kernel(mine_ref, other_ref, best_ref, top_ref, over_ref, out_ref, codes):
    me = lax.axis_index("owner")
    chip = me // 2
    core = me % 2

    @pl.when(is_home(chip))
    def _():
        over = jnp.max(jnp.maximum(fill_codes(other_ref, codes), over_ref[:1]))
        found = [
            jnp.maximum(
                best_ref[:, at : at + 256],
                best_of(other_ref, codes, mine_ref[at : at + 256], top_ref[:1, at : at + 256]),
            )
            for at in range(0, HELD, 256)
        ]
        found = jnp.max(jnp.concatenate(found, axis=1), axis=0, keepdims=True)
        found = jnp.broadcast_to(found, (8, HELD))
        lane = lax.broadcasted_iota(jnp.int32, (1, 128), 1)
        for n, k in enumerate(ORDER):
            start = n * BLOCK
            base = min(start // 128 * 128, HELD - 256)
            size = min(384, HELD - base)
            part = found[:, base : base + size]
            if start > base:
                part = pltpu.roll(part, size - (start - base), 1)
            row = 8 * (2 * (chip ^ k) + core)
            out_ref[pl.ds(row, 1), :] = part[:1, :128]
            out_ref[pl.ds(row + 1, 1), :] = jnp.where(lane >= CAP - 128, over, part[:1, 128:256])


def unpack_kernel(back_ref, slot_ref, best_ref, over_ref):
    core = lax.axis_index("owner") % 2
    rows = slot_ref.shape[1]
    place = lax.broadcasted_iota(jnp.int32, (128, rows), 0)
    row = lax.broadcasted_iota(jnp.int32, (8, 128), 0)
    total = jnp.zeros((8, rows), jnp.float32)
    over = jnp.zeros((8, 128), jnp.float32)
    for n, home in enumerate(HOMES):
        part = back_ref[pl.ds(pl.multiple_of(8 * (2 * home + core), 8), 8), :]
        over = jnp.maximum(over, part)
        for half in range(2):
            value = part[half : half + 1]
            high = value.astype(jnp.bfloat16).astype(jnp.float32)
            middle = (value - high).astype(jnp.bfloat16).astype(jnp.float32)
            low = value - high - middle
            split = jnp.where(row == 0, high, jnp.where(row == 1, middle, jnp.where(row == 2, low, 0.0)))
            hot = (place + 128 * half == slot_ref[n : n + 1]) & (place + 128 * half < BLOCK)
            total = total + jnp.dot(
                split.astype(jnp.bfloat16),
                hot.astype(jnp.float32).astype(jnp.bfloat16),
                preferred_element_type=jnp.float32,
            )
    best_ref[...] = jnp.sum(total, axis=0, keepdims=True)
    over_ref[0, 0] = (over[1, BLOCK - 1 - 128] > 0.0).astype(jnp.int32)


def meet(embeds, clusters, ranks):
    rows, width = embeds.shape
    vmem = pl.BlockSpec(memory_space=pltpu.VMEM)
    params = pltpu.CompilerParams(vmem_limit_bytes=VMEM_LIMIT)
    *sent, slot = pl.pallas_call(
        pack_kernel,
        out_shape=[jax.ShapeDtypeStruct((BLOCK, width), jnp.bfloat16)] * len(HOMES)
        + [jax.ShapeDtypeStruct((8, rows), jnp.int32)],
        in_specs=[vmem] * 3,
        out_specs=[vmem] * (len(HOMES) + 1),
        compiler_params=params,
        name="pack",
    )(embeds, clusters.reshape(1, rows), ranks.reshape(1, rows))
    blocks = {0: sent[0]}
    for k in range(1, CHIPS):
        route = [
            (2 * s + c, 2 * (s ^ k) + c) for s in range(CHIPS) if s ^ k in HOMES for c in range(2)
        ]
        rounds = HOME_ROUNDS if k in HOME_ROUNDS else OUTER_ROUNDS
        blocks[k] = lax.ppermute(sent[rounds.index(k)], "owner", route)
    swap = [(2 * h + c, 2 * h + 1 - c) for h in HOMES for c in range(2)]

    line = jax.ShapeDtypeStruct((8, HELD), jnp.float32)
    codes = [pltpu.VMEM((HELD, 128), jnp.float32)]
    cost = pl.CostEstimate(
        flops=2 * HELD * HELD * width, bytes_accessed=2 * HELD * width, transcendentals=0
    )
    mine = pl.pallas_call(
        join_kernel,
        out_shape=jax.ShapeDtypeStruct((HELD, width), jnp.bfloat16),
        in_specs=[vmem] * CHIPS,
        out_specs=vmem,
        compiler_params=params,
        name="join",
    )(*[blocks[k] for k in ORDER])
    other = lax.ppermute(mine, "owner", swap)
    best, top, over = pl.pallas_call(
        own_kernel,
        out_shape=[line, line, jax.ShapeDtypeStruct((8, 128), jnp.float32)],
        in_specs=[vmem],
        out_specs=[vmem] * 3,
        scratch_shapes=codes,
        compiler_params=params,
        cost_estimate=cost,
        name="own",
    )(mine)
    found = pl.pallas_call(
        other_kernel,
        out_shape=jax.ShapeDtypeStruct((8 * OWNERS, 128), jnp.float32),
        in_specs=[vmem] * 5,
        out_specs=vmem,
        scratch_shapes=codes,
        compiler_params=params,
        cost_estimate=cost,
        name="other",
    )(mine, other, best, top, over)
    back = lax.all_to_all(
        found.reshape(OWNERS, 8, 128), "owner", split_axis=0, concat_axis=0, tiled=True
    )
    best, over = pl.pallas_call(
        unpack_kernel,
        out_shape=[
            jax.ShapeDtypeStruct((1, rows), jnp.float32),
            jax.ShapeDtypeStruct((1, 1), jnp.int32),
        ],
        in_specs=[vmem] * 2,
        out_specs=[vmem, pl.BlockSpec(memory_space=pltpu.SMEM)],
        compiler_params=params,
        name="unpack",
    )(back.reshape(8 * OWNERS, 128), slot)
    return best.reshape(rows), over[0, 0] > 0


def as_sent(array):
    return jax.tree.map(lambda a: a.astype(jnp.bfloat16) if a.dtype == jnp.float32 else a, array)


def from_partner(block, axis, apart):
    count = lax.axis_size(axis)
    route = []
    for low in range(count):
        high = low | 1 << apart
        if high != low and high < count:
            route += [(low, high), (high, low)]
    return lax.ppermute(block, axis, route)


def best_against(best, mine, other):
    mine_unit, mine_cluster, mine_rank = mine
    other_unit, other_cluster, other_rank = other
    query_total = mine_unit.shape[0]
    key_total = other_unit.shape[0]
    query_size = min(512, query_total)
    key_size = min(512, key_total)

    def query_block(query_index, current_best):
        query_start = query_index * query_size
        query_unit = lax.dynamic_slice_in_dim(mine_unit, query_start, query_size, 0)
        query_cluster = lax.dynamic_slice_in_dim(mine_cluster, query_start, query_size, 0)
        query_rank = lax.dynamic_slice_in_dim(mine_rank, query_start, query_size, 0)
        running = lax.dynamic_slice_in_dim(current_best, query_start, query_size, 0)

        def key_block(key_index, running_best):
            key_start = key_index * key_size
            key_unit = lax.dynamic_slice_in_dim(other_unit, key_start, key_size, 0)
            key_cluster = lax.dynamic_slice_in_dim(other_cluster, key_start, key_size, 0)
            key_rank = lax.dynamic_slice_in_dim(other_rank, key_start, key_size, 0)
            allowed = (key_cluster[None, :] == query_cluster[:, None]) & (key_cluster[None, :] >= 0)
            allowed = allowed & (key_rank[None, :] < query_rank[:, None])
            scores = jnp.einsum(
                "qd,kd->qk", query_unit, key_unit, preferred_element_type=jnp.float32
            )
            return jnp.maximum(
                running_best, jnp.max(jnp.where(allowed, scores, jnp.float32(-1.0)), axis=1)
            )

        running = lax.fori_loop(0, key_total // key_size, key_block, running)
        return lax.dynamic_update_slice_in_dim(current_best, running, query_start, 0)

    return lax.fori_loop(0, query_total // query_size, query_block, best)


def route_rows(embeds, clusters, ranks):
    count = lax.axis_size("owner")
    rows, width = embeds.shape
    slots = max(2, 2 * rows // count)
    total = count * slots
    large_cap = total
    values = embeds.astype(jnp.float32)
    unit = (values * lax.rsqrt(jnp.sum(values * values, axis=1, keepdims=True) + 1e-06)).astype(
        jnp.bfloat16
    )
    is_large = clusters >= count
    target = jnp.where(is_large, 8 * (clusters - count) + ranks % 8, clusters)
    positions = jnp.arange(rows, dtype=jnp.int32)
    later = positions[:, None] > positions[None, :]
    earlier = (target[:, None] == target[None, :]) & later
    place = target * slots + jnp.sum(earlier.astype(jnp.int32), axis=1)
    send_unit = jnp.zeros((total, width), jnp.bfloat16).at[place].set(unit)
    send_cluster = jnp.full((total,), -1, jnp.int32).at[place].set(clusters)
    send_rank = jnp.zeros((total,), jnp.int32).at[place].set(ranks)
    got_unit, got_cluster, got_rank = (
        lax.all_to_all(
            send_unit.reshape(count, slots, width), "owner", split_axis=0, concat_axis=0, tiled=True
        ),
        lax.all_to_all(
            send_cluster.reshape(count, slots), "owner", split_axis=0, concat_axis=0, tiled=True
        ),
        lax.all_to_all(
            send_rank.reshape(count, slots), "owner", split_axis=0, concat_axis=0, tiled=True
        ),
    )
    mine = (got_unit.reshape(total, width), got_cluster.reshape(total), got_rank.reshape(total))
    best = jnp.full((total,), -1.0, jnp.float32)
    best = best_against(best, mine, mine)
    large_slot = mine[1] >= count
    large_position = jnp.cumsum(large_slot.astype(jnp.int32)) - 1
    large_place = jnp.where(large_slot, large_position, large_cap)
    large = (
        jnp.zeros((large_cap, width), jnp.bfloat16).at[large_place].set(mine[0], mode="drop"),
        jnp.full((large_cap,), -1, jnp.int32).at[large_place].set(mine[1], mode="drop"),
        jnp.zeros((large_cap,), jnp.int32).at[large_place].set(mine[2], mode="drop"),
    )
    large_best = jnp.full((large_cap,), -1.0, jnp.float32)
    gathered = large
    for level in range(3):
        partner = jax.tree.map(
            lambda part, own: part.astype(own.dtype),
            from_partner(as_sent(gathered), "owner", level),
            gathered,
        )
        large_best = best_against(large_best, large, partner)
        if level < 2:
            gathered = jax.tree.map(
                lambda left, right: jnp.concatenate([left, right], axis=0), gathered, partner
            )
    picked = large_best[jnp.clip(large_position, 0, large_cap - 1)]
    best = jnp.where(large_slot, jnp.maximum(best, picked), best)
    returned = lax.all_to_all(
        best.reshape(count, slots), "owner", split_axis=0, concat_axis=0, tiled=True
    )
    return returned.reshape(total)[place]


def local(embeds, clusters, ranks):
    if lax.axis_size("owner") != OWNERS:
        return route_rows(embeds, clusters, ranks)
    best, over = meet(embeds, clusters, ranks)
    return lax.cond(over, lambda *args: route_rows(*args[:3]), lambda *args: args[3],
                    embeds, clusters, ranks, best)


def solution(mesh):
    return jax.shard_map(
        local,
        mesh=mesh,
        in_specs=(P(("groups", "owner"), None), P(("groups", "owner")), P(("groups", "owner"))),
        out_specs=P(("groups", "owner")),
        check_vma=False,
    )
```

```python
import functools

import jax
import jax.numpy as jnp
from jax import lax
from jax.experimental import pallas as pl
from jax.experimental.pallas import tpu as pltpu
from jax.sharding import PartitionSpec as P

OWNERS = 16
CHIPS = 8
HOMES = (2, 3, 4, 5)
HOME_ROUNDS = (0, 6)
OUTER_ROUNDS = (2, 4)
ORDER = (2,6,4,0)
BLOCK = 160
CAP = 156
META = 16
HELD = CHIPS * BLOCK
VMEM_LIMIT = 48 * 1024 * 1024
NT = (((1,), (1,)), ((), ()))


def is_home(chip):
    return (chip >= HOMES[0]) & (chip <= HOMES[-1])


def pack_kernel(x_ref, cluster_ref, rank_ref, keep_ref, give_ref, slot_ref):
    me = lax.axis_index("owner")
    chip = me // 2
    core = me % 2
    values = x_ref[...].astype(jnp.float32)
    unit = (values * lax.rsqrt(jnp.sum(values * values, axis=1, keepdims=True) + 1e-06)).astype(
        jnp.bfloat16
    )
    rows, width = unit.shape
    cluster = cluster_ref[...]
    rank = rank_ref[...]
    home = jnp.where(
        cluster < OWNERS // 2,
        3,
        jnp.where(cluster < OWNERS, 4, jnp.where(cluster == OWNERS, 2, 5)),
    )
    number = lax.broadcasted_iota(jnp.int32, (8, rows), 0)
    member = number + HOMES[0] == home
    upper = (
        lax.broadcasted_iota(jnp.int32, (rows, rows), 0)
        < lax.broadcasted_iota(jnp.int32, (rows, rows), 1)
    ).astype(jnp.float32).astype(jnp.bfloat16)
    before = jnp.dot(
        member.astype(jnp.float32).astype(jnp.bfloat16), upper, preferred_element_type=jnp.float32
    )
    slot = jnp.where(member, before.astype(jnp.int32), -1)
    slot_ref[...] = slot
    over = (jnp.max(slot) >= CAP).astype(jnp.float32)
    line = lax.broadcasted_iota(jnp.int32, (META, rows), 0)
    first = META - (BLOCK - CAP)
    meta = jnp.where(
        line == first,
        cluster + 1,
        jnp.where(line == first + 1, rank >> 6, jnp.where(line == first + 2, rank & 63, 0)),
    )
    meta = meta.astype(jnp.float32).astype(jnp.bfloat16)
    place = lax.broadcasted_iota(jnp.int32, (256, rows), 0)
    for n in range(4):
        out_ref, to_core, at = (keep_ref, give_ref)[n // 2], core ^ (n // 2), n % 2 * BLOCK
        k = jnp.where(is_home(chip), HOME_ROUNDS[n % 2], OUTER_ROUNDS[n % 2]) | to_core
        mine = slot_ref[pl.ds((chip ^ k) - HOMES[0], 1), :]
        hot = ((place == mine) & (place < CAP)).astype(jnp.float32).astype(jnp.bfloat16)
        block = jnp.dot(hot[:BLOCK], unit, preferred_element_type=jnp.float32)
        out_ref[at : at + BLOCK] = block.astype(jnp.bfloat16)
        tail = lax.dot_general(meta, hot, NT, preferred_element_type=jnp.float32)
        row = lax.broadcasted_iota(jnp.int32, (META, 256), 0)
        tail = jnp.where(row == META - 1, over, tail)
        tail = jnp.where(row >= first, tail, block[BLOCK - META :, :256])
        out_ref[at + BLOCK - META : at + BLOCK, :256] = tail.astype(jnp.bfloat16)


def fill_codes(keys, codes):
    eye = (
        lax.broadcasted_iota(jnp.int32, (BLOCK, 256), 0)
        == lax.broadcasted_iota(jnp.int32, (BLOCK, 256), 1)
    ).astype(jnp.float32).astype(jnp.bfloat16)
    lane = lax.broadcasted_iota(jnp.int32, (1, META), 1)
    first = META - (BLOCK - CAP)
    scale = jnp.where(
        lane == first, 4096.0, jnp.where(lane == first + 1, 64.0, jnp.where(lane == first + 2, 1.0, 0.0))
    )
    over = jnp.zeros((1, 128), jnp.float32)
    for n in range(CHIPS):
        meta = keys[(n + 1) * BLOCK - META : (n + 1) * BLOCK, :256]
        over = jnp.maximum(over, meta[META - 1 :, :128].astype(jnp.float32))
        columns = lax.dot_general(eye, meta, NT, preferred_element_type=jnp.float32)
        code = jnp.sum(columns * scale, axis=1, keepdims=True)
        codes[n * BLOCK : (n + 1) * BLOCK] = jnp.broadcast_to(code, (BLOCK, 128))
    return over


def best_of(keys, codes, query, top):
    size = query.shape[0]
    step = HELD // 2
    base = jnp.floor(top * (1.0 / 4096.0)) * 4096.0
    best = jnp.full((8, size), -1.0, jnp.float32)
    for start in range(0, HELD, step):
        score = lax.dot_general(
            keys[start : start + step], query, NT, preferred_element_type=jnp.float32
        )
        code = jnp.concatenate([codes[start : start + step]] * (size // 128), axis=1)
        score = jnp.where((code >= base) & (code < top), score, -1.0)
        best = jnp.maximum(best, jnp.max(score.reshape(step // 8, 8, size), axis=0))
    return best


def pair_kernel(keep_ref, got_ref, first_ref, second_ref):
    first_ref[:BLOCK] = keep_ref[:BLOCK]
    first_ref[BLOCK:] = got_ref[:BLOCK]
    second_ref[:BLOCK] = keep_ref[BLOCK:]
    second_ref[BLOCK:] = got_ref[BLOCK:]


def join_kernel(mine_ref, *refs):
    blocks, out_ref = refs[:-1], refs[-1]
    for n, ref in enumerate(blocks):
        out_ref[n * 2 * BLOCK : (n + 1) * 2 * BLOCK] = ref[...]

    @pl.when(lax.axis_index("owner") % 2 == 0)
    def _():
        at = ORDER.index(0) * 2 * BLOCK
        out_ref[at : at + 2 * BLOCK] = mine_ref[...]


def own_kernel(mine_ref, best_ref, top_ref, over_ref, codes):
    @pl.when(is_home(lax.axis_index("owner") // 2))
    def _():
        over_ref[...] = jnp.broadcast_to(fill_codes(mine_ref, codes), over_ref.shape)
        for at in range(0, HELD, 256):
            top = jnp.transpose(codes[at : at + 256])[:8]
            top_ref[:, at : at + 256] = top
            best_ref[:, at : at + 256] = best_of(
                mine_ref, codes, mine_ref[at : at + 256], top[:1]
            )


def other_kernel(mine_ref, other_ref, best_ref, top_ref, over_ref, out_ref, codes):
    me = lax.axis_index("owner")
    chip = me // 2
    core = me % 2

    @pl.when(is_home(chip))
    def _():
        over = jnp.max(jnp.maximum(fill_codes(other_ref, codes), over_ref[:1]))
        found = [
            jnp.maximum(
                best_ref[:, at : at + 256],
                best_of(other_ref, codes, mine_ref[at : at + 256], top_ref[:1, at : at + 256]),
            )
            for at in range(0, HELD, 256)
        ]
        found = jnp.max(jnp.concatenate(found, axis=1), axis=0, keepdims=True)
        found = jnp.broadcast_to(found, (8, HELD))
        lane = lax.broadcasted_iota(jnp.int32, (1, 128), 1)
        for n in range(CHIPS):
            start = n * BLOCK
            to_chip = chip ^ (ORDER[n // 2] | core)
            to_core = core ^ (n % 2)
            base = min(start // 128 * 128, HELD - 256)
            size = min(384, HELD - base)
            part = found[:, base : base + size]
            if start > base:
                part = pltpu.roll(part, size - (start - base), 1)
            row = 8 * (2 * to_chip + to_core)
            out_ref[pl.ds(row, 1), :] = part[:1, :128]
            out_ref[pl.ds(row + 1, 1), :] = jnp.where(lane >= CAP - 128, over, part[:1, 128:256])


def unpack_kernel(back_ref, slot_ref, best_ref, over_ref):
    chip = lax.axis_index("owner") // 2
    rows = slot_ref.shape[1]
    place = lax.broadcasted_iota(jnp.int32, (128, rows), 0)
    row = lax.broadcasted_iota(jnp.int32, (8, 128), 0)
    total = jnp.zeros((8, rows), jnp.float32)
    over = jnp.zeros((8, 128), jnp.float32)
    for n, home in enumerate(HOMES):
        held = 2 * home + ((chip ^ home) & 1)
        part = back_ref[pl.ds(pl.multiple_of(8 * held, 8), 8), :]
        over = jnp.maximum(over, part)
        for half in range(2):
            value = part[half : half + 1]
            high = value.astype(jnp.bfloat16).astype(jnp.float32)
            middle = (value - high).astype(jnp.bfloat16).astype(jnp.float32)
            low = value - high - middle
            split = jnp.where(row == 0, high, jnp.where(row == 1, middle, jnp.where(row == 2, low, 0.0)))
            hot = (place + 128 * half == slot_ref[n : n + 1]) & (place + 128 * half < BLOCK)
            total = total + jnp.dot(
                split.astype(jnp.bfloat16),
                hot.astype(jnp.float32).astype(jnp.bfloat16),
                preferred_element_type=jnp.float32,
            )
    best_ref[...] = jnp.sum(total, axis=0, keepdims=True)
    over_ref[0, 0] = (over[1, BLOCK - 1 - 128] > 0.0).astype(jnp.int32)


def meet(embeds, clusters, ranks):
    rows, width = embeds.shape
    vmem = pl.BlockSpec(memory_space=pltpu.VMEM)
    params = pltpu.CompilerParams(vmem_limit_bytes=VMEM_LIMIT)
    two_blocks = jax.ShapeDtypeStruct((2 * BLOCK, width), jnp.bfloat16)
    keep, give, slot = pl.pallas_call(
        pack_kernel,
        out_shape=[two_blocks, two_blocks, jax.ShapeDtypeStruct((8, rows), jnp.int32)],
        in_specs=[vmem] * 3,
        out_specs=[vmem] * 3,
        compiler_params=params,
        name="pack",
    )(embeds, clusters.reshape(1, rows), ranks.reshape(1, rows))
    got = lax.ppermute(give, "owner", [(n, n ^ 1) for n in range(OWNERS)])
    first, second = pl.pallas_call(
        pair_kernel,
        out_shape=[two_blocks] * 2,
        in_specs=[vmem] * 2,
        out_specs=[vmem] * 2,
        compiler_params=params,
        name="pair",
    )(keep, got)

    def carry(pair, k, cores=(0, 1)):
        chips = [s for s in range(CHIPS) if (s in HOMES) == (k in HOME_ROUNDS)]
        return lax.ppermute(
            pair, "owner", [(2 * s + c, 2 * (s ^ (k | c)) + c) for s in chips for c in cores]
        )

    pairs = {6: carry(second, 6), 4: carry(second, 4), 2: carry(first, 2), 0: carry(first, 0, (1,))}
    swap = [(2 * h + c, 2 * h + 1 - c) for h in HOMES for c in range(2)]
    line = jax.ShapeDtypeStruct((8, HELD), jnp.float32)
    codes = [pltpu.VMEM((HELD, 128), jnp.float32)]
    cost = pl.CostEstimate(
        flops=2 * HELD * HELD * width, bytes_accessed=2 * HELD * width, transcendentals=0
    )
    mine = pl.pallas_call(
        join_kernel,
        out_shape=jax.ShapeDtypeStruct((HELD, width), jnp.bfloat16),
        in_specs=[vmem] * (1 + len(ORDER)),
        out_specs=vmem,
        compiler_params=params,
        name="join",
    )(first, *[pairs[k] for k in ORDER])
    other = lax.ppermute(mine, "owner", swap)
    best, top, over = pl.pallas_call(
        own_kernel,
        out_shape=[line, line, jax.ShapeDtypeStruct((8, 128), jnp.float32)],
        in_specs=[vmem],
        out_specs=[vmem] * 3,
        scratch_shapes=codes,
        compiler_params=params,
        cost_estimate=cost,
        name="own",
    )(mine)
    found = pl.pallas_call(
        other_kernel,
        out_shape=jax.ShapeDtypeStruct((8 * OWNERS, 128), jnp.float32),
        in_specs=[vmem] * 5,
        out_specs=vmem,
        scratch_shapes=codes,
        compiler_params=params,
        cost_estimate=cost,
        name="other",
    )(mine, other, best, top, over)
    back = lax.all_to_all(
        found.reshape(OWNERS, 8, 128), "owner", split_axis=0, concat_axis=0, tiled=True
    )
    best, over = pl.pallas_call(
        unpack_kernel,
        out_shape=[
            jax.ShapeDtypeStruct((1, rows), jnp.float32),
            jax.ShapeDtypeStruct((1, 1), jnp.int32),
        ],
        in_specs=[vmem] * 2,
        out_specs=[vmem, pl.BlockSpec(memory_space=pltpu.SMEM)],
        compiler_params=params,
        name="unpack",
    )(back.reshape(8 * OWNERS, 128), slot)
    return best.reshape(rows), over[0, 0] > 0


def as_sent(array):
    return jax.tree.map(lambda a: a.astype(jnp.bfloat16) if a.dtype == jnp.float32 else a, array)


def from_partner(block, axis, apart):
    count = lax.axis_size(axis)
    route = []
    for low in range(count):
        high = low | 1 << apart
        if high != low and high < count:
            route += [(low, high), (high, low)]
    return lax.ppermute(block, axis, route)


def best_against(best, mine, other):
    mine_unit, mine_cluster, mine_rank = mine
    other_unit, other_cluster, other_rank = other
    query_total = mine_unit.shape[0]
    key_total = other_unit.shape[0]
    query_size = min(512, query_total)
    key_size = min(512, key_total)

    def query_block(query_index, current_best):
        query_start = query_index * query_size
        query_unit = lax.dynamic_slice_in_dim(mine_unit, query_start, query_size, 0)
        query_cluster = lax.dynamic_slice_in_dim(mine_cluster, query_start, query_size, 0)
        query_rank = lax.dynamic_slice_in_dim(mine_rank, query_start, query_size, 0)
        running = lax.dynamic_slice_in_dim(current_best, query_start, query_size, 0)

        def key_block(key_index, running_best):
            key_start = key_index * key_size
            key_unit = lax.dynamic_slice_in_dim(other_unit, key_start, key_size, 0)
            key_cluster = lax.dynamic_slice_in_dim(other_cluster, key_start, key_size, 0)
            key_rank = lax.dynamic_slice_in_dim(other_rank, key_start, key_size, 0)
            allowed = (key_cluster[None, :] == query_cluster[:, None]) & (key_cluster[None, :] >= 0)
            allowed = allowed & (key_rank[None, :] < query_rank[:, None])
            scores = jnp.einsum(
                "qd,kd->qk", query_unit, key_unit, preferred_element_type=jnp.float32
            )
            return jnp.maximum(
                running_best, jnp.max(jnp.where(allowed, scores, jnp.float32(-1.0)), axis=1)
            )

        running = lax.fori_loop(0, key_total // key_size, key_block, running)
        return lax.dynamic_update_slice_in_dim(current_best, running, query_start, 0)

    return lax.fori_loop(0, query_total // query_size, query_block, best)


def route_rows(embeds, clusters, ranks):
    count = lax.axis_size("owner")
    rows, width = embeds.shape
    slots = max(2, 2 * rows // count)
    total = count * slots
    large_cap = total
    values = embeds.astype(jnp.float32)
    unit = (values * lax.rsqrt(jnp.sum(values * values, axis=1, keepdims=True) + 1e-06)).astype(
        jnp.bfloat16
    )
    is_large = clusters >= count
    target = jnp.where(is_large, 8 * (clusters - count) + ranks % 8, clusters)
    positions = jnp.arange(rows, dtype=jnp.int32)
    later = positions[:, None] > positions[None, :]
    earlier = (target[:, None] == target[None, :]) & later
    place = target * slots + jnp.sum(earlier.astype(jnp.int32), axis=1)
    send_unit = jnp.zeros((total, width), jnp.bfloat16).at[place].set(unit)
    send_cluster = jnp.full((total,), -1, jnp.int32).at[place].set(clusters)
    send_rank = jnp.zeros((total,), jnp.int32).at[place].set(ranks)
    got_unit, got_cluster, got_rank = (
        lax.all_to_all(
            send_unit.reshape(count, slots, width), "owner", split_axis=0, concat_axis=0, tiled=True
        ),
        lax.all_to_all(
            send_cluster.reshape(count, slots), "owner", split_axis=0, concat_axis=0, tiled=True
        ),
        lax.all_to_all(
            send_rank.reshape(count, slots), "owner", split_axis=0, concat_axis=0, tiled=True
        ),
    )
    mine = (got_unit.reshape(total, width), got_cluster.reshape(total), got_rank.reshape(total))
    best = jnp.full((total,), -1.0, jnp.float32)
    best = best_against(best, mine, mine)
    large_slot = mine[1] >= count
    large_position = jnp.cumsum(large_slot.astype(jnp.int32)) - 1
    large_place = jnp.where(large_slot, large_position, large_cap)
    large = (
        jnp.zeros((large_cap, width), jnp.bfloat16).at[large_place].set(mine[0], mode="drop"),
        jnp.full((large_cap,), -1, jnp.int32).at[large_place].set(mine[1], mode="drop"),
        jnp.zeros((large_cap,), jnp.int32).at[large_place].set(mine[2], mode="drop"),
    )
    large_best = jnp.full((large_cap,), -1.0, jnp.float32)
    gathered = large
    for level in range(3):
        partner = jax.tree.map(
            lambda part, own: part.astype(own.dtype),
            from_partner(as_sent(gathered), "owner", level),
            gathered,
        )
        large_best = best_against(large_best, large, partner)
        if level < 2:
            gathered = jax.tree.map(
                lambda left, right: jnp.concatenate([left, right], axis=0), gathered, partner
            )
    picked = large_best[jnp.clip(large_position, 0, large_cap - 1)]
    best = jnp.where(large_slot, jnp.maximum(best, picked), best)
    returned = lax.all_to_all(
        best.reshape(count, slots), "owner", split_axis=0, concat_axis=0, tiled=True
    )
    return returned.reshape(total)[place]


def local(embeds, clusters, ranks):
    if lax.axis_size("owner") != OWNERS:
        return route_rows(embeds, clusters, ranks)
    best, over = meet(embeds, clusters, ranks)
    return lax.cond(over, lambda *args: route_rows(*args[:3]), lambda *args: args[3],
                    embeds, clusters, ranks, best)


def solution(mesh):
    return jax.shard_map(
        local,
        mesh=mesh,
        in_specs=(P(("groups", "owner"), None), P(("groups", "owner")), P(("groups", "owner"))),
        out_specs=P(("groups", "owner")),
        check_vma=False,
    )
```

```python
import functools

import jax
import jax.numpy as jnp
from jax import lax
from jax.experimental import pallas as pl
from jax.experimental.pallas import tpu as pltpu
from jax.sharding import PartitionSpec as P

OWNERS = 16
CHIPS = 8
HOMES = (2, 3, 4, 5)
HOME_ROUNDS = (0, 6)
OUTER_ROUNDS = (2, 4)
ORDER = (2,6,4,0)
BLOCK = 160
CAP = 156
META = 16
HELD = CHIPS * BLOCK
VMEM_LIMIT = 48 * 1024 * 1024
NT = (((1,), (1,)), ((), ()))


def is_home(chip):
    return (chip >= HOMES[0]) & (chip <= HOMES[-1])


def pack_rows(unit_ref, meta_ref, slot_ref, chip, to_core, out_ref):
    rows = slot_ref.shape[1]
    first = META - (BLOCK - CAP)
    place = lax.broadcasted_iota(jnp.int32, (256, rows), 0)
    over = (jnp.max(slot_ref[...]) >= CAP).astype(jnp.float32)
    for n in range(2):
        at = n * BLOCK
        k = jnp.where(is_home(chip), HOME_ROUNDS[n], OUTER_ROUNDS[n]) | to_core
        mine = slot_ref[pl.ds((chip ^ k) - HOMES[0], 1), :]
        hot = ((place == mine) & (place < CAP)).astype(jnp.float32).astype(jnp.bfloat16)
        block = jnp.dot(hot[:BLOCK], unit_ref[...], preferred_element_type=jnp.float32)
        out_ref[at : at + BLOCK] = block.astype(jnp.bfloat16)
        tail = lax.dot_general(meta_ref[...], hot, NT, preferred_element_type=jnp.float32)
        row = lax.broadcasted_iota(jnp.int32, (META, 256), 0)
        tail = jnp.where(row == META - 1, over, tail)
        tail = jnp.where(row >= first, tail, block[BLOCK - META :, :256])
        out_ref[at + BLOCK - META : at + BLOCK, :256] = tail.astype(jnp.bfloat16)


def pack_kernel(x_ref, cluster_ref, rank_ref, give_ref, slot_ref, unit_ref, meta_ref):
    me = lax.axis_index("owner")
    chip = me // 2
    core = me % 2
    values = x_ref[...].astype(jnp.float32)
    unit = (values * lax.rsqrt(jnp.sum(values * values, axis=1, keepdims=True) + 1e-06)).astype(
        jnp.bfloat16
    )
    rows, width = unit.shape
    cluster = cluster_ref[...]
    rank = rank_ref[...]
    home = jnp.where(
        cluster < OWNERS // 2,
        3,
        jnp.where(cluster < OWNERS, 4, jnp.where(cluster == OWNERS, 2, 5)),
    )
    number = lax.broadcasted_iota(jnp.int32, (8, rows), 0)
    member = number + HOMES[0] == home
    upper = (
        lax.broadcasted_iota(jnp.int32, (rows, rows), 0)
        < lax.broadcasted_iota(jnp.int32, (rows, rows), 1)
    ).astype(jnp.float32).astype(jnp.bfloat16)
    before = jnp.dot(
        member.astype(jnp.float32).astype(jnp.bfloat16), upper, preferred_element_type=jnp.float32
    )
    slot = jnp.where(member, before.astype(jnp.int32), -1)
    slot_ref[...] = slot
    line = lax.broadcasted_iota(jnp.int32, (META, rows), 0)
    first = META - (BLOCK - CAP)
    meta = jnp.where(
        line == first,
        cluster + 1,
        jnp.where(line == first + 1, rank >> 6, jnp.where(line == first + 2, rank & 63, 0)),
    )
    meta = meta.astype(jnp.float32).astype(jnp.bfloat16)
    unit_ref[...] = unit
    meta_ref[...] = meta
    pack_rows(unit_ref, meta_ref, slot_ref, chip, core ^ 1, give_ref)


def keep_kernel(unit_ref, meta_ref, slot_ref, keep_ref):
    me = lax.axis_index("owner")
    pack_rows(unit_ref, meta_ref, slot_ref, me // 2, me % 2, keep_ref)


def fill_codes(keys, codes):
    eye = (
        lax.broadcasted_iota(jnp.int32, (BLOCK, 256), 0)
        == lax.broadcasted_iota(jnp.int32, (BLOCK, 256), 1)
    ).astype(jnp.float32).astype(jnp.bfloat16)
    lane = lax.broadcasted_iota(jnp.int32, (1, META), 1)
    first = META - (BLOCK - CAP)
    scale = jnp.where(
        lane == first, 4096.0, jnp.where(lane == first + 1, 64.0, jnp.where(lane == first + 2, 1.0, 0.0))
    )
    over = jnp.zeros((1, 128), jnp.float32)
    for n in range(CHIPS):
        meta = keys[(n + 1) * BLOCK - META : (n + 1) * BLOCK, :256]
        over = jnp.maximum(over, meta[META - 1 :, :128].astype(jnp.float32))
        columns = lax.dot_general(eye, meta, NT, preferred_element_type=jnp.float32)
        code = jnp.sum(columns * scale, axis=1, keepdims=True)
        codes[n * BLOCK : (n + 1) * BLOCK] = jnp.broadcast_to(code, (BLOCK, 128))
    return over


def best_of(keys, codes, query, top):
    size = query.shape[0]
    step = HELD // 2
    base = jnp.floor(top * (1.0 / 4096.0)) * 4096.0
    best = jnp.full((8, size), -1.0, jnp.float32)
    for start in range(0, HELD, step):
        score = lax.dot_general(
            keys[start : start + step], query, NT, preferred_element_type=jnp.float32
        )
        code = jnp.concatenate([codes[start : start + step]] * (size // 128), axis=1)
        score = jnp.where((code >= base) & (code < top), score, -1.0)
        best = jnp.maximum(best, jnp.max(score.reshape(step // 8, 8, size), axis=0))
    return best


def pair_kernel(keep_ref, got_ref, first_ref, second_ref):
    first_ref[:BLOCK] = keep_ref[:BLOCK]
    first_ref[BLOCK:] = got_ref[:BLOCK]
    second_ref[:BLOCK] = keep_ref[BLOCK:]
    second_ref[BLOCK:] = got_ref[BLOCK:]


def join_kernel(mine_ref, *refs):
    blocks, out_ref = refs[:-1], refs[-1]
    for n, ref in enumerate(blocks):
        out_ref[n * 2 * BLOCK : (n + 1) * 2 * BLOCK] = ref[...]

    @pl.when(lax.axis_index("owner") % 2 == 0)
    def _():
        at = ORDER.index(0) * 2 * BLOCK
        out_ref[at : at + 2 * BLOCK] = mine_ref[...]


def own_kernel(mine_ref, best_ref, top_ref, over_ref, codes):
    @pl.when(is_home(lax.axis_index("owner") // 2))
    def _():
        over_ref[...] = jnp.broadcast_to(fill_codes(mine_ref, codes), over_ref.shape)
        for at in range(0, HELD, 256):
            top = jnp.transpose(codes[at : at + 256])[:8]
            top_ref[:, at : at + 256] = top
            best_ref[:, at : at + 256] = best_of(
                mine_ref, codes, mine_ref[at : at + 256], top[:1]
            )


def other_kernel(mine_ref, other_ref, best_ref, top_ref, over_ref, out_ref, codes):
    me = lax.axis_index("owner")
    chip = me // 2
    core = me % 2

    @pl.when(is_home(chip))
    def _():
        over = jnp.max(jnp.maximum(fill_codes(other_ref, codes), over_ref[:1]))
        found = [
            jnp.maximum(
                best_ref[:, at : at + 256],
                best_of(other_ref, codes, mine_ref[at : at + 256], top_ref[:1, at : at + 256]),
            )
            for at in range(0, HELD, 256)
        ]
        found = jnp.max(jnp.concatenate(found, axis=1), axis=0, keepdims=True)
        found = jnp.broadcast_to(found, (8, HELD))
        lane = lax.broadcasted_iota(jnp.int32, (1, 128), 1)
        for n in range(CHIPS):
            start = n * BLOCK
            to_chip = chip ^ (ORDER[n // 2] | core)
            to_core = core ^ (n % 2)
            base = min(start // 128 * 128, HELD - 256)
            size = min(384, HELD - base)
            part = found[:, base : base + size]
            if start > base:
                part = pltpu.roll(part, size - (start - base), 1)
            row = 8 * (2 * to_chip + to_core)
            out_ref[pl.ds(row, 1), :] = part[:1, :128]
            out_ref[pl.ds(row + 1, 1), :] = jnp.where(lane >= CAP - 128, over, part[:1, 128:256])


def unpack_kernel(back_ref, slot_ref, best_ref, over_ref):
    chip = lax.axis_index("owner") // 2
    rows = slot_ref.shape[1]
    place = lax.broadcasted_iota(jnp.int32, (128, rows), 0)
    row = lax.broadcasted_iota(jnp.int32, (8, 128), 0)
    total = jnp.zeros((8, rows), jnp.float32)
    over = jnp.zeros((8, 128), jnp.float32)
    for n, home in enumerate(HOMES):
        held = 2 * home + ((chip ^ home) & 1)
        part = back_ref[pl.ds(pl.multiple_of(8 * held, 8), 8), :]
        over = jnp.maximum(over, part)
        for half in range(2):
            value = part[half : half + 1]
            high = value.astype(jnp.bfloat16).astype(jnp.float32)
            middle = (value - high).astype(jnp.bfloat16).astype(jnp.float32)
            low = value - high - middle
            split = jnp.where(row == 0, high, jnp.where(row == 1, middle, jnp.where(row == 2, low, 0.0)))
            hot = (place + 128 * half == slot_ref[n : n + 1]) & (place + 128 * half < BLOCK)
            total = total + jnp.dot(
                split.astype(jnp.bfloat16),
                hot.astype(jnp.float32).astype(jnp.bfloat16),
                preferred_element_type=jnp.float32,
            )
    best_ref[...] = jnp.sum(total, axis=0, keepdims=True)
    over_ref[0, 0] = (over[1, BLOCK - 1 - 128] > 0.0).astype(jnp.int32)


def meet(embeds, clusters, ranks):
    rows, width = embeds.shape
    vmem = pl.BlockSpec(memory_space=pltpu.VMEM)
    params = pltpu.CompilerParams(vmem_limit_bytes=VMEM_LIMIT)
    two_blocks = jax.ShapeDtypeStruct((2 * BLOCK, width), jnp.bfloat16)
    give, slot, unit, meta = pl.pallas_call(
        pack_kernel,
        out_shape=[
            two_blocks,
            jax.ShapeDtypeStruct((8, rows), jnp.int32),
            jax.ShapeDtypeStruct((rows, width), jnp.bfloat16),
            jax.ShapeDtypeStruct((META, rows), jnp.bfloat16),
        ],
        in_specs=[vmem] * 3,
        out_specs=[vmem] * 4,
        compiler_params=params,
        name="pack",
    )(embeds, clusters.reshape(1, rows), ranks.reshape(1, rows))
    got = lax.ppermute(give, "owner", [(n, n ^ 1) for n in range(OWNERS)])
    keep = pl.pallas_call(
        keep_kernel,
        out_shape=two_blocks,
        in_specs=[vmem] * 3,
        out_specs=vmem,
        compiler_params=params,
        cost_estimate=pl.CostEstimate(
            flops=4 * BLOCK * rows * width, bytes_accessed=4 * rows * width, transcendentals=0
        ),
        name="keep",
    )(unit, meta, slot)
    first, second = pl.pallas_call(
        pair_kernel,
        out_shape=[two_blocks] * 2,
        in_specs=[vmem] * 2,
        out_specs=[vmem] * 2,
        compiler_params=params,
        name="pair",
    )(keep, got)

    def carry(pair, k, cores=(0, 1)):
        chips = [s for s in range(CHIPS) if (s in HOMES) == (k in HOME_ROUNDS)]
        return lax.ppermute(
            pair, "owner", [(2 * s + c, 2 * (s ^ (k | c)) + c) for s in chips for c in cores]
        )

    pairs = {6: carry(second, 6), 4: carry(second, 4), 2: carry(first, 2), 0: carry(first, 0, (1,))}
    swap = [(2 * h + c, 2 * h + 1 - c) for h in HOMES for c in range(2)]
    line = jax.ShapeDtypeStruct((8, HELD), jnp.float32)
    codes = [pltpu.VMEM((HELD, 128), jnp.float32)]
    cost = pl.CostEstimate(
        flops=2 * HELD * HELD * width, bytes_accessed=2 * HELD * width, transcendentals=0
    )
    mine = pl.pallas_call(
        join_kernel,
        out_shape=jax.ShapeDtypeStruct((HELD, width), jnp.bfloat16),
        in_specs=[vmem] * (1 + len(ORDER)),
        out_specs=vmem,
        compiler_params=params,
        name="join",
    )(first, *[pairs[k] for k in ORDER])
    other = lax.ppermute(mine, "owner", swap)
    best, top, over = pl.pallas_call(
        own_kernel,
        out_shape=[line, line, jax.ShapeDtypeStruct((8, 128), jnp.float32)],
        in_specs=[vmem],
        out_specs=[vmem] * 3,
        scratch_shapes=codes,
        compiler_params=params,
        cost_estimate=cost,
        name="own",
    )(mine)
    found = pl.pallas_call(
        other_kernel,
        out_shape=jax.ShapeDtypeStruct((8 * OWNERS, 128), jnp.float32),
        in_specs=[vmem] * 5,
        out_specs=vmem,
        scratch_shapes=codes,
        compiler_params=params,
        cost_estimate=cost,
        name="other",
    )(mine, other, best, top, over)
    back = lax.all_to_all(
        found.reshape(OWNERS, 8, 128), "owner", split_axis=0, concat_axis=0, tiled=True
    )
    best, over = pl.pallas_call(
        unpack_kernel,
        out_shape=[
            jax.ShapeDtypeStruct((1, rows), jnp.float32),
            jax.ShapeDtypeStruct((1, 1), jnp.int32),
        ],
        in_specs=[vmem] * 2,
        out_specs=[vmem, pl.BlockSpec(memory_space=pltpu.SMEM)],
        compiler_params=params,
        name="unpack",
    )(back.reshape(8 * OWNERS, 128), slot)
    return best.reshape(rows), over[0, 0] > 0


def as_sent(array):
    return jax.tree.map(lambda a: a.astype(jnp.bfloat16) if a.dtype == jnp.float32 else a, array)


def from_partner(block, axis, apart):
    count = lax.axis_size(axis)
    route = []
    for low in range(count):
        high = low | 1 << apart
        if high != low and high < count:
            route += [(low, high), (high, low)]
    return lax.ppermute(block, axis, route)


def best_against(best, mine, other):
    mine_unit, mine_cluster, mine_rank = mine
    other_unit, other_cluster, other_rank = other
    query_total = mine_unit.shape[0]
    key_total = other_unit.shape[0]
    query_size = min(512, query_total)
    key_size = min(512, key_total)

    def query_block(query_index, current_best):
        query_start = query_index * query_size
        query_unit = lax.dynamic_slice_in_dim(mine_unit, query_start, query_size, 0)
        query_cluster = lax.dynamic_slice_in_dim(mine_cluster, query_start, query_size, 0)
        query_rank = lax.dynamic_slice_in_dim(mine_rank, query_start, query_size, 0)
        running = lax.dynamic_slice_in_dim(current_best, query_start, query_size, 0)

        def key_block(key_index, running_best):
            key_start = key_index * key_size
            key_unit = lax.dynamic_slice_in_dim(other_unit, key_start, key_size, 0)
            key_cluster = lax.dynamic_slice_in_dim(other_cluster, key_start, key_size, 0)
            key_rank = lax.dynamic_slice_in_dim(other_rank, key_start, key_size, 0)
            allowed = (key_cluster[None, :] == query_cluster[:, None]) & (key_cluster[None, :] >= 0)
            allowed = allowed & (key_rank[None, :] < query_rank[:, None])
            scores = jnp.einsum(
                "qd,kd->qk", query_unit, key_unit, preferred_element_type=jnp.float32
            )
            return jnp.maximum(
                running_best, jnp.max(jnp.where(allowed, scores, jnp.float32(-1.0)), axis=1)
            )

        running = lax.fori_loop(0, key_total // key_size, key_block, running)
        return lax.dynamic_update_slice_in_dim(current_best, running, query_start, 0)

    return lax.fori_loop(0, query_total // query_size, query_block, best)


def route_rows(embeds, clusters, ranks):
    count = lax.axis_size("owner")
    rows, width = embeds.shape
    slots = max(2, 2 * rows // count)
    total = count * slots
    large_cap = total
    values = embeds.astype(jnp.float32)
    unit = (values * lax.rsqrt(jnp.sum(values * values, axis=1, keepdims=True) + 1e-06)).astype(
        jnp.bfloat16
    )
    is_large = clusters >= count
    target = jnp.where(is_large, 8 * (clusters - count) + ranks % 8, clusters)
    positions = jnp.arange(rows, dtype=jnp.int32)
    later = positions[:, None] > positions[None, :]
    earlier = (target[:, None] == target[None, :]) & later
    place = target * slots + jnp.sum(earlier.astype(jnp.int32), axis=1)
    send_unit = jnp.zeros((total, width), jnp.bfloat16).at[place].set(unit)
    send_cluster = jnp.full((total,), -1, jnp.int32).at[place].set(clusters)
    send_rank = jnp.zeros((total,), jnp.int32).at[place].set(ranks)
    got_unit, got_cluster, got_rank = (
        lax.all_to_all(
            send_unit.reshape(count, slots, width), "owner", split_axis=0, concat_axis=0, tiled=True
        ),
        lax.all_to_all(
            send_cluster.reshape(count, slots), "owner", split_axis=0, concat_axis=0, tiled=True
        ),
        lax.all_to_all(
            send_rank.reshape(count, slots), "owner", split_axis=0, concat_axis=0, tiled=True
        ),
    )
    mine = (got_unit.reshape(total, width), got_cluster.reshape(total), got_rank.reshape(total))
    best = jnp.full((total,), -1.0, jnp.float32)
    best = best_against(best, mine, mine)
    large_slot = mine[1] >= count
    large_position = jnp.cumsum(large_slot.astype(jnp.int32)) - 1
    large_place = jnp.where(large_slot, large_position, large_cap)
    large = (
        jnp.zeros((large_cap, width), jnp.bfloat16).at[large_place].set(mine[0], mode="drop"),
        jnp.full((large_cap,), -1, jnp.int32).at[large_place].set(mine[1], mode="drop"),
        jnp.zeros((large_cap,), jnp.int32).at[large_place].set(mine[2], mode="drop"),
    )
    large_best = jnp.full((large_cap,), -1.0, jnp.float32)
    gathered = large
    for level in range(3):
        partner = jax.tree.map(
            lambda part, own: part.astype(own.dtype),
            from_partner(as_sent(gathered), "owner", level),
            gathered,
        )
        large_best = best_against(large_best, large, partner)
        if level < 2:
            gathered = jax.tree.map(
                lambda left, right: jnp.concatenate([left, right], axis=0), gathered, partner
            )
    picked = large_best[jnp.clip(large_position, 0, large_cap - 1)]
    best = jnp.where(large_slot, jnp.maximum(best, picked), best)
    returned = lax.all_to_all(
        best.reshape(count, slots), "owner", split_axis=0, concat_axis=0, tiled=True
    )
    return returned.reshape(total)[place]


def local(embeds, clusters, ranks):
    if lax.axis_size("owner") != OWNERS:
        return route_rows(embeds, clusters, ranks)
    best, over = meet(embeds, clusters, ranks)
    return lax.cond(over, lambda *args: route_rows(*args[:3]), lambda *args: args[3],
                    embeds, clusters, ranks, best)


def solution(mesh):
    return jax.shard_map(
        local,
        mesh=mesh,
        in_specs=(P(("groups", "owner"), None), P(("groups", "owner")), P(("groups", "owner"))),
        out_specs=P(("groups", "owner")),
        check_vma=False,
    )
```

```python
import functools

import jax
import jax.numpy as jnp
from jax import lax
from jax.experimental import pallas as pl
from jax.experimental.pallas import tpu as pltpu
from jax.sharding import PartitionSpec as P

OWNERS = 16
CHIPS = 8
HOMES = (2, 3, 4, 5)
HOME_ROUNDS = (0, 6)
OUTER_ROUNDS = (2, 4)
ORDER = (2, 6, 4, 0)
BLOCK = 160
CAP = 156
META = 16
HELD = CHIPS * BLOCK
VMEM_LIMIT = 28 * 1024 * 1024
NT = (((1,), (1,)), ((), ()))


def is_home(chip):
    return (chip >= HOMES[0]) & (chip <= HOMES[-1])


def pack_rows(unit_ref, meta_ref, slot_ref, chip, to_core, out_ref):
    rows = slot_ref.shape[1]
    first = META - (BLOCK - CAP)
    place = lax.broadcasted_iota(jnp.int32, (256, rows), 0)
    over = (jnp.max(slot_ref[...]) >= CAP).astype(jnp.float32)
    for n in range(2):
        at = n * BLOCK
        k = jnp.where(is_home(chip), HOME_ROUNDS[n], OUTER_ROUNDS[n]) | to_core
        mine = slot_ref[pl.ds((chip ^ k) - HOMES[0], 1), :]
        hot = ((place == mine) & (place < CAP)).astype(jnp.float32).astype(jnp.bfloat16)
        block = jnp.dot(hot[:BLOCK], unit_ref[...], preferred_element_type=jnp.float32)
        out_ref[at : at + BLOCK] = block.astype(jnp.bfloat16)
        tail = lax.dot_general(meta_ref[...], hot, NT, preferred_element_type=jnp.float32)
        row = lax.broadcasted_iota(jnp.int32, (META, 256), 0)
        tail = jnp.where(row == META - 1, over, tail)
        tail = jnp.where(row >= first, tail, block[BLOCK - META :, :256])
        out_ref[at + BLOCK - META : at + BLOCK, :256] = tail.astype(jnp.bfloat16)


def pack_kernel(x_ref, cluster_ref, rank_ref, give_ref, slot_ref, unit_ref, meta_ref):
    me = lax.axis_index("owner")
    chip = me // 2
    core = me % 2
    values = x_ref[...].astype(jnp.float32)
    unit = (values * lax.rsqrt(jnp.sum(values * values, axis=1, keepdims=True) + 1e-06)).astype(
        jnp.bfloat16
    )
    rows, width = unit.shape
    cluster = cluster_ref[...]
    rank = rank_ref[...]
    home = jnp.where(
        cluster < OWNERS // 2,
        3,
        jnp.where(cluster < OWNERS, 4, jnp.where(cluster == OWNERS, 2, 5)),
    )
    number = lax.broadcasted_iota(jnp.int32, (8, rows), 0)
    member = number + HOMES[0] == home
    upper = (
        lax.broadcasted_iota(jnp.int32, (rows, rows), 0)
        < lax.broadcasted_iota(jnp.int32, (rows, rows), 1)
    ).astype(jnp.float32).astype(jnp.bfloat16)
    before = jnp.dot(
        member.astype(jnp.float32).astype(jnp.bfloat16), upper, preferred_element_type=jnp.float32
    )
    slot = jnp.where(member, before.astype(jnp.int32), -1)
    slot_ref[...] = slot
    line = lax.broadcasted_iota(jnp.int32, (META, rows), 0)
    first = META - (BLOCK - CAP)
    meta = jnp.where(
        line == first,
        cluster + 1,
        jnp.where(line == first + 1, rank >> 6, jnp.where(line == first + 2, rank & 63, 0)),
    )
    meta = meta.astype(jnp.float32).astype(jnp.bfloat16)
    unit_ref[...] = unit
    meta_ref[...] = meta
    pack_rows(unit_ref, meta_ref, slot_ref, chip, core ^ 1, give_ref)


def keep_kernel(unit_ref, meta_ref, slot_ref, keep_ref):
    me = lax.axis_index("owner")
    pack_rows(unit_ref, meta_ref, slot_ref, me // 2, me % 2, keep_ref)


def fill_codes(keys, codes, blocks):
    eye = (
        lax.broadcasted_iota(jnp.int32, (BLOCK, 256), 0)
        == lax.broadcasted_iota(jnp.int32, (BLOCK, 256), 1)
    ).astype(jnp.float32).astype(jnp.bfloat16)
    lane = lax.broadcasted_iota(jnp.int32, (1, META), 1)
    first = META - (BLOCK - CAP)
    scale = jnp.where(
        lane == first, 4096.0, jnp.where(lane == first + 1, 64.0, jnp.where(lane == first + 2, 1.0, 0.0))
    )
    over = jnp.zeros((1, 128), jnp.float32)
    for n in range(blocks):
        meta = keys[(n + 1) * BLOCK - META : (n + 1) * BLOCK, :256]
        over = jnp.maximum(over, meta[META - 1 :, :128].astype(jnp.float32))
        columns = lax.dot_general(eye, meta, NT, preferred_element_type=jnp.float32)
        code = jnp.sum(columns * scale, axis=1, keepdims=True)
        codes[n * BLOCK : (n + 1) * BLOCK] = jnp.broadcast_to(code, (BLOCK, 128))
    return over


def best_of(keys, codes, query, top):
    size = query.shape[0]
    total = keys.shape[0]
    step = total // 2
    base = jnp.floor(top * (1.0 / 4096.0)) * 4096.0
    best = jnp.full((8, size), -1.0, jnp.float32)
    for start in range(0, total, step):
        score = lax.dot_general(
            keys[start : start + step], query, NT, preferred_element_type=jnp.float32
        )
        code = jnp.concatenate([codes[start : start + step]] * (size // 128), axis=1)
        score = jnp.where((code >= base) & (code < top), score, -1.0)
        best = jnp.maximum(best, jnp.max(score.reshape(step // 8, 8, size), axis=0))
    return best


def pair_kernel(keep_ref, got_ref, first_ref, second_ref):
    first_ref[:BLOCK] = keep_ref[:BLOCK]
    first_ref[BLOCK:] = got_ref[:BLOCK]
    second_ref[:BLOCK] = keep_ref[BLOCK:]
    second_ref[BLOCK:] = got_ref[BLOCK:]


def halve_kernel(pair_ref, one_ref, two_ref):
    one_ref[...] = pair_ref[:BLOCK]
    two_ref[...] = pair_ref[BLOCK:]


def join_kernel(mine_ref, one_ref, two_ref, *refs):
    blocks, (out_ref, late_ref) = refs[:-2], refs[-2:]
    for n, ref in enumerate(blocks):
        out_ref[n * 2 * BLOCK : (n + 1) * 2 * BLOCK] = ref[...]

    @pl.when(lax.axis_index("owner") % 2 == 0)
    def _():
        at = ORDER.index(0) * 2 * BLOCK
        out_ref[at : at + 2 * BLOCK] = mine_ref[...]

    out_ref[HELD : HELD + BLOCK] = one_ref[...]
    out_ref[HELD + BLOCK :] = two_ref[...]
    late_ref[...] = out_ref[2 * BLOCK : HELD]


def own_kernel(mine_ref, best_ref, top_ref, over_ref, codes):
    @pl.when(is_home(lax.axis_index("owner") // 2))
    def _():
        over_ref[...] = jnp.broadcast_to(fill_codes(mine_ref, codes, CHIPS + 2), over_ref.shape)
        for at in range(0, HELD, 256):
            top = jnp.transpose(codes[at : at + 256])[:8]
            top_ref[:, at : at + 256] = top
            best_ref[:, at : at + 256] = best_of(
                mine_ref, codes, mine_ref[at : at + 256], top[:1]
            )


def other_kernel(mine_ref, other_ref, best_ref, top_ref, over_ref, out_ref, codes):
    me = lax.axis_index("owner")
    chip = me // 2
    core = me % 2

    @pl.when(is_home(chip))
    def _():
        over = jnp.max(jnp.maximum(fill_codes(other_ref, codes, CHIPS - 2), over_ref[:1]))
        found = [
            jnp.maximum(
                best_ref[:, at : at + 256],
                best_of(other_ref, codes, mine_ref[at : at + 256], top_ref[:1, at : at + 256]),
            )
            for at in range(0, HELD, 256)
        ]
        found = jnp.max(jnp.concatenate(found, axis=1), axis=0, keepdims=True)
        found = jnp.broadcast_to(found, (8, HELD))
        lane = lax.broadcasted_iota(jnp.int32, (1, 128), 1)
        for n in range(CHIPS):
            start = n * BLOCK
            to_chip = chip ^ (ORDER[n // 2] | core)
            to_core = core ^ (n % 2)
            base = min(start // 128 * 128, HELD - 256)
            size = min(384, HELD - base)
            part = found[:, base : base + size]
            if start > base:
                part = pltpu.roll(part, size - (start - base), 1)
            row = 8 * (2 * to_chip + to_core)
            out_ref[pl.ds(row, 1), :] = part[:1, :128]
            out_ref[pl.ds(row + 1, 1), :] = jnp.where(lane >= CAP - 128, over, part[:1, 128:256])


def unpack_kernel(back_ref, slot_ref, best_ref, over_ref):
    chip = lax.axis_index("owner") // 2
    rows = slot_ref.shape[1]
    place = lax.broadcasted_iota(jnp.int32, (128, rows), 0)
    row = lax.broadcasted_iota(jnp.int32, (8, 128), 0)
    total = jnp.zeros((8, rows), jnp.float32)
    over = jnp.zeros((8, 128), jnp.float32)
    for n, home in enumerate(HOMES):
        held = 2 * home + ((chip ^ home) & 1)
        part = back_ref[pl.ds(pl.multiple_of(8 * held, 8), 8), :]
        over = jnp.maximum(over, part)
        for half in range(2):
            value = part[half : half + 1]
            high = value.astype(jnp.bfloat16).astype(jnp.float32)
            middle = (value - high).astype(jnp.bfloat16).astype(jnp.float32)
            low = value - high - middle
            split = jnp.where(row == 0, high, jnp.where(row == 1, middle, jnp.where(row == 2, low, 0.0)))
            hot = (place + 128 * half == slot_ref[n : n + 1]) & (place + 128 * half < BLOCK)
            total = total + jnp.dot(
                split.astype(jnp.bfloat16),
                hot.astype(jnp.float32).astype(jnp.bfloat16),
                preferred_element_type=jnp.float32,
            )
    best_ref[...] = jnp.sum(total, axis=0, keepdims=True)
    over_ref[0, 0] = (over[1, BLOCK - 1 - 128] > 0.0).astype(jnp.int32)


def meet(embeds, clusters, ranks):
    rows, width = embeds.shape
    vmem = pl.BlockSpec(memory_space=pltpu.VMEM)
    params = pltpu.CompilerParams(vmem_limit_bytes=VMEM_LIMIT)
    two_blocks = jax.ShapeDtypeStruct((2 * BLOCK, width), jnp.bfloat16)
    give, slot, unit, meta = pl.pallas_call(
        pack_kernel,
        out_shape=[
            two_blocks,
            jax.ShapeDtypeStruct((8, rows), jnp.int32),
            jax.ShapeDtypeStruct((rows, width), jnp.bfloat16),
            jax.ShapeDtypeStruct((META, rows), jnp.bfloat16),
        ],
        in_specs=[vmem] * 3,
        out_specs=[vmem] * 4,
        compiler_params=params,
        name="pack",
    )(embeds, clusters.reshape(1, rows), ranks.reshape(1, rows))
    got = lax.ppermute(give, "owner", [(n, n ^ 1) for n in range(OWNERS)])
    keep = pl.pallas_call(
        keep_kernel,
        out_shape=two_blocks,
        in_specs=[vmem] * 3,
        out_specs=vmem,
        compiler_params=params,
        cost_estimate=pl.CostEstimate(
            flops=4 * BLOCK * rows * width, bytes_accessed=4 * rows * width, transcendentals=0
        ),
        name="keep",
    )(unit, meta, slot)
    first, second = pl.pallas_call(
        pair_kernel,
        out_shape=[two_blocks] * 2,
        in_specs=[vmem] * 2,
        out_specs=[vmem] * 2,
        compiler_params=params,
        name="pair",
    )(keep, got)

    def carry(pair, k, cores=(0, 1)):
        chips = [s for s in range(CHIPS) if (s in HOMES) == (k in HOME_ROUNDS)]
        return lax.ppermute(
            pair, "owner", [(2 * s + c, 2 * (s ^ (k | c)) + c) for s in chips for c in cores]
        )

    pairs = {6: carry(second, 6), 4: carry(second, 4), 2: carry(first, 2), 0: carry(first, 0, (1,))}
    swap = [(2 * h + c, 2 * h + 1 - c) for h in HOMES for c in range(2)]
    line = jax.ShapeDtypeStruct((8, HELD), jnp.float32)
    codes = [pltpu.VMEM((HELD + 2 * BLOCK, 128), jnp.float32)]
    cost = pl.CostEstimate(
        flops=2 * HELD * HELD * width, bytes_accessed=2 * HELD * width, transcendentals=0
    )
    halves = pl.pallas_call(
        halve_kernel,
        out_shape=[jax.ShapeDtypeStruct((BLOCK, width), jnp.bfloat16)] * 2,
        in_specs=[vmem],
        out_specs=[vmem] * 2,
        compiler_params=params,
        name="halve",
    )(pairs[2])
    halves = [lax.ppermute(block, "owner", swap) for block in halves]
    mine, late = pl.pallas_call(
        join_kernel,
        out_shape=[
            jax.ShapeDtypeStruct((HELD + 2 * BLOCK, width), jnp.bfloat16),
            jax.ShapeDtypeStruct((HELD - 2 * BLOCK, width), jnp.bfloat16),
        ],
        in_specs=[vmem] * (3 + len(ORDER)),
        out_specs=[vmem] * 2,
        compiler_params=params,
        name="join",
    )(first, *halves, *[pairs[k] for k in ORDER])
    other = lax.ppermute(late, "owner", swap)
    best, top, over = pl.pallas_call(
        own_kernel,
        out_shape=[line, line, jax.ShapeDtypeStruct((8, 128), jnp.float32)],
        in_specs=[vmem],
        out_specs=[vmem] * 3,
        scratch_shapes=codes,
        compiler_params=params,
        cost_estimate=cost,
        name="own",
    )(mine)
    found = pl.pallas_call(
        other_kernel,
        out_shape=jax.ShapeDtypeStruct((8 * OWNERS, 128), jnp.float32),
        in_specs=[vmem] * 5,
        out_specs=vmem,
        scratch_shapes=codes,
        compiler_params=params,
        cost_estimate=cost,
        name="other",
    )(mine, other, best, top, over)
    back = lax.all_to_all(
        found.reshape(OWNERS, 8, 128), "owner", split_axis=0, concat_axis=0, tiled=True
    )
    best, over = pl.pallas_call(
        unpack_kernel,
        out_shape=[
            jax.ShapeDtypeStruct((1, rows), jnp.float32),
            jax.ShapeDtypeStruct((1, 1), jnp.int32),
        ],
        in_specs=[vmem] * 2,
        out_specs=[vmem, pl.BlockSpec(memory_space=pltpu.SMEM)],
        compiler_params=params,
        name="unpack",
    )(back.reshape(8 * OWNERS, 128), slot)
    return best.reshape(rows), over[0, 0] > 0


def as_sent(array):
    return jax.tree.map(lambda a: a.astype(jnp.bfloat16) if a.dtype == jnp.float32 else a, array)


def from_partner(block, axis, apart):
    count = lax.axis_size(axis)
    route = []
    for low in range(count):
        high = low | 1 << apart
        if high != low and high < count:
            route += [(low, high), (high, low)]
    return lax.ppermute(block, axis, route)


def best_against(best, mine, other):
    mine_unit, mine_cluster, mine_rank = mine
    other_unit, other_cluster, other_rank = other
    query_total = mine_unit.shape[0]
    key_total = other_unit.shape[0]
    query_size = min(512, query_total)
    key_size = min(512, key_total)

    def query_block(query_index, current_best):
        query_start = query_index * query_size
        query_unit = lax.dynamic_slice_in_dim(mine_unit, query_start, query_size, 0)
        query_cluster = lax.dynamic_slice_in_dim(mine_cluster, query_start, query_size, 0)
        query_rank = lax.dynamic_slice_in_dim(mine_rank, query_start, query_size, 0)
        running = lax.dynamic_slice_in_dim(current_best, query_start, query_size, 0)

        def key_block(key_index, running_best):
            key_start = key_index * key_size
            key_unit = lax.dynamic_slice_in_dim(other_unit, key_start, key_size, 0)
            key_cluster = lax.dynamic_slice_in_dim(other_cluster, key_start, key_size, 0)
            key_rank = lax.dynamic_slice_in_dim(other_rank, key_start, key_size, 0)
            allowed = (key_cluster[None, :] == query_cluster[:, None]) & (key_cluster[None, :] >= 0)
            allowed = allowed & (key_rank[None, :] < query_rank[:, None])
            scores = jnp.einsum(
                "qd,kd->qk", query_unit, key_unit, preferred_element_type=jnp.float32
            )
            return jnp.maximum(
                running_best, jnp.max(jnp.where(allowed, scores, jnp.float32(-1.0)), axis=1)
            )

        running = lax.fori_loop(0, key_total // key_size, key_block, running)
        return lax.dynamic_update_slice_in_dim(current_best, running, query_start, 0)

    return lax.fori_loop(0, query_total // query_size, query_block, best)


def route_rows(embeds, clusters, ranks):
    count = lax.axis_size("owner")
    rows, width = embeds.shape
    slots = max(2, 2 * rows // count)
    total = count * slots
    large_cap = total
    values = embeds.astype(jnp.float32)
    unit = (values * lax.rsqrt(jnp.sum(values * values, axis=1, keepdims=True) + 1e-06)).astype(
        jnp.bfloat16
    )
    is_large = clusters >= count
    target = jnp.where(is_large, 8 * (clusters - count) + ranks % 8, clusters)
    positions = jnp.arange(rows, dtype=jnp.int32)
    later = positions[:, None] > positions[None, :]
    earlier = (target[:, None] == target[None, :]) & later
    place = target * slots + jnp.sum(earlier.astype(jnp.int32), axis=1)
    send_unit = jnp.zeros((total, width), jnp.bfloat16).at[place].set(unit)
    send_cluster = jnp.full((total,), -1, jnp.int32).at[place].set(clusters)
    send_rank = jnp.zeros((total,), jnp.int32).at[place].set(ranks)
    got_unit, got_cluster, got_rank = (
        lax.all_to_all(
            send_unit.reshape(count, slots, width), "owner", split_axis=0, concat_axis=0, tiled=True
        ),
        lax.all_to_all(
            send_cluster.reshape(count, slots), "owner", split_axis=0, concat_axis=0, tiled=True
        ),
        lax.all_to_all(
            send_rank.reshape(count, slots), "owner", split_axis=0, concat_axis=0, tiled=True
        ),
    )
    mine = (got_unit.reshape(total, width), got_cluster.reshape(total), got_rank.reshape(total))
    best = jnp.full((total,), -1.0, jnp.float32)
    best = best_against(best, mine, mine)
    large_slot = mine[1] >= count
    large_position = jnp.cumsum(large_slot.astype(jnp.int32)) - 1
    large_place = jnp.where(large_slot, large_position, large_cap)
    large = (
        jnp.zeros((large_cap, width), jnp.bfloat16).at[large_place].set(mine[0], mode="drop"),
        jnp.full((large_cap,), -1, jnp.int32).at[large_place].set(mine[1], mode="drop"),
        jnp.zeros((large_cap,), jnp.int32).at[large_place].set(mine[2], mode="drop"),
    )
    large_best = jnp.full((large_cap,), -1.0, jnp.float32)
    gathered = large
    for level in range(3):
        partner = jax.tree.map(
            lambda part, own: part.astype(own.dtype),
            from_partner(as_sent(gathered), "owner", level),
            gathered,
        )
        large_best = best_against(large_best, large, partner)
        if level < 2:
            gathered = jax.tree.map(
                lambda left, right: jnp.concatenate([left, right], axis=0), gathered, partner
            )
    picked = large_best[jnp.clip(large_position, 0, large_cap - 1)]
    best = jnp.where(large_slot, jnp.maximum(best, picked), best)
    returned = lax.all_to_all(
        best.reshape(count, slots), "owner", split_axis=0, concat_axis=0, tiled=True
    )
    return returned.reshape(total)[place]


def local(embeds, clusters, ranks):
    if lax.axis_size("owner") != OWNERS:
        return route_rows(embeds, clusters, ranks)
    best, over = meet(embeds, clusters, ranks)
    return lax.cond(over, lambda *args: route_rows(*args[:3]), lambda *args: args[3],
                    embeds, clusters, ranks, best)


def solution(mesh):
    return jax.shard_map(
        local,
        mesh=mesh,
        in_specs=(P(("groups", "owner"), None), P(("groups", "owner")), P(("groups", "owner"))),
        out_specs=P(("groups", "owner")),
        check_vma=False,
    )
```

```python
import functools

import jax
import jax.numpy as jnp
from jax import lax
from jax.experimental import pallas as pl
from jax.experimental.pallas import tpu as pltpu
from jax.sharding import PartitionSpec as P

OWNERS = 16
CHIPS = 8
HOMES = (2, 3, 4, 5)
HOME_ROUNDS = (0, 6)
OUTER_ROUNDS = (2, 4)
ORDER = (2, 6, 4, 0)
BLOCK = 160
CAP = 156
META = 16
HELD = CHIPS * BLOCK
VMEM_LIMIT = 28 * 1024 * 1024
NT = (((1,), (1,)), ((), ()))


def is_home(chip):
    return (chip >= HOMES[0]) & (chip <= HOMES[-1])


def pack_rows(unit_ref, meta_ref, slot_ref, chip, to_core, out_ref):
    rows = slot_ref.shape[1]
    first = META - (BLOCK - CAP)
    place = lax.broadcasted_iota(jnp.int32, (256, rows), 0)
    over = (jnp.max(slot_ref[...]) >= CAP).astype(jnp.float32)
    for n in range(2):
        at = n * BLOCK
        k = jnp.where(is_home(chip), HOME_ROUNDS[n], OUTER_ROUNDS[n]) | to_core
        mine = slot_ref[pl.ds((chip ^ k) - HOMES[0], 1), :]
        hot = ((place == mine) & (place < CAP)).astype(jnp.float32).astype(jnp.bfloat16)
        block = jnp.dot(hot[:BLOCK], unit_ref[...], preferred_element_type=jnp.float32)
        out_ref[at : at + BLOCK] = block.astype(jnp.bfloat16)
        tail = lax.dot_general(meta_ref[...], hot, NT, preferred_element_type=jnp.float32)
        row = lax.broadcasted_iota(jnp.int32, (META, 256), 0)
        tail = jnp.where(row == META - 1, over, tail)
        tail = jnp.where(row >= first, tail, block[BLOCK - META :, :256])
        out_ref[at + BLOCK - META : at + BLOCK, :256] = tail.astype(jnp.bfloat16)


def pack_kernel(x_ref, cluster_ref, rank_ref, give_ref, slot_ref, unit_ref, meta_ref):
    me = lax.axis_index("owner")
    chip = me // 2
    core = me % 2
    values = x_ref[...].astype(jnp.float32)
    unit = (values * lax.rsqrt(jnp.sum(values * values, axis=1, keepdims=True) + 1e-06)).astype(
        jnp.bfloat16
    )
    rows, width = unit.shape
    cluster = cluster_ref[...]
    rank = rank_ref[...]
    home = jnp.where(
        cluster < OWNERS // 2,
        3,
        jnp.where(cluster < OWNERS, 4, jnp.where(cluster == OWNERS, 2, 5)),
    )
    number = lax.broadcasted_iota(jnp.int32, (8, rows), 0)
    member = number + HOMES[0] == home
    upper = (
        lax.broadcasted_iota(jnp.int32, (rows, rows), 0)
        < lax.broadcasted_iota(jnp.int32, (rows, rows), 1)
    ).astype(jnp.float32).astype(jnp.bfloat16)
    before = jnp.dot(
        member.astype(jnp.float32).astype(jnp.bfloat16), upper, preferred_element_type=jnp.float32
    )
    slot = jnp.where(member, before.astype(jnp.int32), -1)
    slot_ref[...] = slot
    line = lax.broadcasted_iota(jnp.int32, (META, rows), 0)
    first = META - (BLOCK - CAP)
    meta = jnp.where(
        line == first,
        cluster + 1,
        jnp.where(line == first + 1, rank >> 6, jnp.where(line == first + 2, rank & 63, 0)),
    )
    meta = meta.astype(jnp.float32).astype(jnp.bfloat16)
    unit_ref[...] = unit
    meta_ref[...] = meta
    pack_rows(unit_ref, meta_ref, slot_ref, chip, core ^ 1, give_ref)


def keep_kernel(unit_ref, meta_ref, slot_ref, keep_ref):
    me = lax.axis_index("owner")
    pack_rows(unit_ref, meta_ref, slot_ref, me // 2, me % 2, keep_ref)


def fill_codes(keys, codes, blocks):
    eye = (
        lax.broadcasted_iota(jnp.int32, (BLOCK, 256), 0)
        == lax.broadcasted_iota(jnp.int32, (BLOCK, 256), 1)
    ).astype(jnp.float32).astype(jnp.bfloat16)
    lane = lax.broadcasted_iota(jnp.int32, (1, META), 1)
    first = META - (BLOCK - CAP)
    scale = jnp.where(
        lane == first, 4096.0, jnp.where(lane == first + 1, 64.0, jnp.where(lane == first + 2, 1.0, 0.0))
    )
    over = jnp.zeros((1, 128), jnp.float32)
    for n in range(blocks):
        meta = keys[(n + 1) * BLOCK - META : (n + 1) * BLOCK, :256]
        over = jnp.maximum(over, meta[META - 1 :, :128].astype(jnp.float32))
        columns = lax.dot_general(eye, meta, NT, preferred_element_type=jnp.float32)
        code = jnp.sum(columns * scale, axis=1, keepdims=True)
        codes[n * BLOCK : (n + 1) * BLOCK] = jnp.broadcast_to(code, (BLOCK, 128))
    return over


def best_of(keys, codes, query, top, first=0):
    size = query.shape[0]
    total = keys.shape[0]
    step = (total - first) // 2
    base = jnp.floor(top * (1.0 / 4096.0)) * 4096.0
    best = jnp.full((8, size), -1.0, jnp.float32)
    for start in range(first, total, step):
        score = lax.dot_general(
            keys[start : start + step], query, NT, preferred_element_type=jnp.float32
        )
        code = jnp.concatenate([codes[start : start + step]] * (size // 128), axis=1)
        score = jnp.where((code >= base) & (code < top), score, -1.0)
        best = jnp.maximum(best, jnp.max(score.reshape(step // 8, 8, size), axis=0))
    return best


def pair_kernel(keep_ref, got_ref, first_ref, second_ref):
    first_ref[:BLOCK] = keep_ref[:BLOCK]
    first_ref[BLOCK:] = got_ref[:BLOCK]
    second_ref[:BLOCK] = keep_ref[BLOCK:]
    second_ref[BLOCK:] = got_ref[BLOCK:]


def halve_kernel(pair_ref, one_ref, two_ref):
    one_ref[...] = pair_ref[:BLOCK]
    two_ref[...] = pair_ref[BLOCK:]


def early_kernel(pair_ref, one_ref, two_ref, best_ref, keys, codes):
    @pl.when(is_home(lax.axis_index("owner") // 2))
    def _():
        keys[: 2 * BLOCK] = pair_ref[...]
        keys[2 * BLOCK : 3 * BLOCK] = one_ref[...]
        keys[3 * BLOCK :] = two_ref[...]
        fill_codes(keys, codes, 4)
        top = jnp.transpose(codes[:256])[:1]
        best_ref[...] = best_of(keys, codes, keys[:256], top)


def join_kernel(mine_ref, one_ref, two_ref, early_ref, *refs):
    blocks, (out_ref, late_ref, known_ref) = refs[:-3], refs[-3:]
    known_ref[...] = early_ref[...]
    for n, ref in enumerate(blocks):
        out_ref[n * 2 * BLOCK : (n + 1) * 2 * BLOCK] = ref[...]

    @pl.when(lax.axis_index("owner") % 2 == 0)
    def _():
        at = ORDER.index(0) * 2 * BLOCK
        out_ref[at : at + 2 * BLOCK] = mine_ref[...]

    out_ref[HELD : HELD + BLOCK] = one_ref[...]
    out_ref[HELD + BLOCK :] = two_ref[...]
    late_ref[...] = out_ref[2 * BLOCK : HELD]


def own_kernel(mine_ref, early_ref, late_ref, best_ref, top_ref, over_ref, codes):
    @pl.when(is_home(lax.axis_index("owner") // 2))
    def _():
        over_ref[...] = jnp.broadcast_to(fill_codes(mine_ref, codes, CHIPS + 2), over_ref.shape)
        late_codes = codes.at[pl.ds(2 * BLOCK, HELD - 2 * BLOCK)]
        for at in range(0, HELD, 256):
            top = jnp.transpose(codes[at : at + 256])[:8]
            top_ref[:, at : at + 256] = top
            if at == 0:
                own = best_of(late_ref, late_codes, mine_ref[:256], top[:1])
                best_ref[:, :256] = jnp.maximum(early_ref[...], own)
            else:
                best_ref[:, at : at + 256] = best_of(
                    mine_ref, codes, mine_ref[at : at + 256], top[:1]
                )


def other_kernel(mine_ref, other_ref, best_ref, top_ref, over_ref, out_ref, codes):
    me = lax.axis_index("owner")
    chip = me // 2
    core = me % 2

    @pl.when(is_home(chip))
    def _():
        over = jnp.max(jnp.maximum(fill_codes(other_ref, codes, CHIPS - 2), over_ref[:1]))
        found = [
            jnp.maximum(
                best_ref[:, at : at + 256],
                best_of(other_ref, codes, mine_ref[at : at + 256], top_ref[:1, at : at + 256]),
            )
            for at in range(0, HELD, 256)
        ]
        found = jnp.max(jnp.concatenate(found, axis=1), axis=0, keepdims=True)
        found = jnp.broadcast_to(found, (8, HELD))
        lane = lax.broadcasted_iota(jnp.int32, (1, 128), 1)
        for n in range(CHIPS):
            start = n * BLOCK
            to_chip = chip ^ (ORDER[n // 2] | core)
            to_core = core ^ (n % 2)
            base = min(start // 128 * 128, HELD - 256)
            size = min(384, HELD - base)
            part = found[:, base : base + size]
            if start > base:
                part = pltpu.roll(part, size - (start - base), 1)
            row = 8 * (2 * to_chip + to_core)
            out_ref[pl.ds(row, 1), :] = part[:1, :128]
            out_ref[pl.ds(row + 1, 1), :] = jnp.where(lane >= CAP - 128, over, part[:1, 128:256])


def unpack_kernel(back_ref, slot_ref, best_ref, over_ref):
    chip = lax.axis_index("owner") // 2
    rows = slot_ref.shape[1]
    place = lax.broadcasted_iota(jnp.int32, (128, rows), 0)
    row = lax.broadcasted_iota(jnp.int32, (8, 128), 0)
    total = jnp.zeros((8, rows), jnp.float32)
    over = jnp.zeros((8, 128), jnp.float32)
    for n, home in enumerate(HOMES):
        held = 2 * home + ((chip ^ home) & 1)
        part = back_ref[pl.ds(pl.multiple_of(8 * held, 8), 8), :]
        over = jnp.maximum(over, part)
        for half in range(2):
            value = part[half : half + 1]
            high = value.astype(jnp.bfloat16).astype(jnp.float32)
            middle = (value - high).astype(jnp.bfloat16).astype(jnp.float32)
            low = value - high - middle
            split = jnp.where(row == 0, high, jnp.where(row == 1, middle, jnp.where(row == 2, low, 0.0)))
            hot = (place + 128 * half == slot_ref[n : n + 1]) & (place + 128 * half < BLOCK)
            total = total + jnp.dot(
                split.astype(jnp.bfloat16),
                hot.astype(jnp.float32).astype(jnp.bfloat16),
                preferred_element_type=jnp.float32,
            )
    best_ref[...] = jnp.sum(total, axis=0, keepdims=True)
    over_ref[0, 0] = (over[1, BLOCK - 1 - 128] > 0.0).astype(jnp.int32)


def meet(embeds, clusters, ranks):
    rows, width = embeds.shape
    vmem = pl.BlockSpec(memory_space=pltpu.VMEM)
    params = pltpu.CompilerParams(vmem_limit_bytes=VMEM_LIMIT)
    two_blocks = jax.ShapeDtypeStruct((2 * BLOCK, width), jnp.bfloat16)
    give, slot, unit, meta = pl.pallas_call(
        pack_kernel,
        out_shape=[
            two_blocks,
            jax.ShapeDtypeStruct((8, rows), jnp.int32),
            jax.ShapeDtypeStruct((rows, width), jnp.bfloat16),
            jax.ShapeDtypeStruct((META, rows), jnp.bfloat16),
        ],
        in_specs=[vmem] * 3,
        out_specs=[vmem] * 4,
        compiler_params=params,
        name="pack",
    )(embeds, clusters.reshape(1, rows), ranks.reshape(1, rows))
    got = lax.ppermute(give, "owner", [(n, n ^ 1) for n in range(OWNERS)])
    keep = pl.pallas_call(
        keep_kernel,
        out_shape=two_blocks,
        in_specs=[vmem] * 3,
        out_specs=vmem,
        compiler_params=params,
        cost_estimate=pl.CostEstimate(
            flops=4 * BLOCK * rows * width, bytes_accessed=4 * rows * width, transcendentals=0
        ),
        name="keep",
    )(unit, meta, slot)
    first, second = pl.pallas_call(
        pair_kernel,
        out_shape=[two_blocks] * 2,
        in_specs=[vmem] * 2,
        out_specs=[vmem] * 2,
        compiler_params=params,
        name="pair",
    )(keep, got)

    def carry(pair, k, cores=(0, 1)):
        chips = [s for s in range(CHIPS) if (s in HOMES) == (k in HOME_ROUNDS)]
        return lax.ppermute(
            pair, "owner", [(2 * s + c, 2 * (s ^ (k | c)) + c) for s in chips for c in cores]
        )

    pairs = {6: carry(second, 6), 4: carry(second, 4), 2: carry(first, 2), 0: carry(first, 0, (1,))}
    swap = [(2 * h + c, 2 * h + 1 - c) for h in HOMES for c in range(2)]
    line = jax.ShapeDtypeStruct((8, HELD), jnp.float32)
    codes = [pltpu.VMEM((HELD + 2 * BLOCK, 128), jnp.float32)]
    cost = pl.CostEstimate(
        flops=2 * HELD * HELD * width, bytes_accessed=2 * HELD * width, transcendentals=0
    )
    halves = pl.pallas_call(
        halve_kernel,
        out_shape=[jax.ShapeDtypeStruct((BLOCK, width), jnp.bfloat16)] * 2,
        in_specs=[vmem],
        out_specs=[vmem] * 2,
        compiler_params=params,
        name="halve",
    )(pairs[2])
    halves = [lax.ppermute(block, "owner", swap) for block in halves]
    early = pl.pallas_call(
        early_kernel,
        out_shape=jax.ShapeDtypeStruct((8, 256), jnp.float32),
        in_specs=[vmem] * 3,
        out_specs=vmem,
        scratch_shapes=[
            pltpu.VMEM((4 * BLOCK, width), jnp.bfloat16),
            pltpu.VMEM((4 * BLOCK, 128), jnp.float32),
        ],
        compiler_params=params,
        cost_estimate=pl.CostEstimate(flops=0, bytes_accessed=0, transcendentals=0),
        name="early",
    )(pairs[2], *halves)
    mine, late, early = pl.pallas_call(
        join_kernel,
        out_shape=[
            jax.ShapeDtypeStruct((HELD + 2 * BLOCK, width), jnp.bfloat16),
            jax.ShapeDtypeStruct((HELD - 2 * BLOCK, width), jnp.bfloat16),
            jax.ShapeDtypeStruct((8, 256), jnp.float32),
        ],
        in_specs=[vmem] * (4 + len(ORDER)),
        out_specs=[vmem] * 3,
        compiler_params=params,
        name="join",
    )(first, *halves, early, *[pairs[k] for k in ORDER])
    other = lax.ppermute(late, "owner", swap)
    best, top, over = pl.pallas_call(
        own_kernel,
        out_shape=[line, line, jax.ShapeDtypeStruct((8, 128), jnp.float32)],
        in_specs=[vmem] * 3,
        out_specs=[vmem] * 3,
        scratch_shapes=codes,
        compiler_params=params,
        cost_estimate=cost,
        name="own",
    )(mine, early, late)
    found = pl.pallas_call(
        other_kernel,
        out_shape=jax.ShapeDtypeStruct((8 * OWNERS, 128), jnp.float32),
        in_specs=[vmem] * 5,
        out_specs=vmem,
        scratch_shapes=codes,
        compiler_params=params,
        cost_estimate=cost,
        name="other",
    )(mine, other, best, top, over)
    back = lax.all_to_all(
        found.reshape(OWNERS, 8, 128), "owner", split_axis=0, concat_axis=0, tiled=True
    )
    best, over = pl.pallas_call(
        unpack_kernel,
        out_shape=[
            jax.ShapeDtypeStruct((1, rows), jnp.float32),
            jax.ShapeDtypeStruct((1, 1), jnp.int32),
        ],
        in_specs=[vmem] * 2,
        out_specs=[vmem, pl.BlockSpec(memory_space=pltpu.SMEM)],
        compiler_params=params,
        name="unpack",
    )(back.reshape(8 * OWNERS, 128), slot)
    return best.reshape(rows), over[0, 0] > 0


def as_sent(array):
    return jax.tree.map(lambda a: a.astype(jnp.bfloat16) if a.dtype == jnp.float32 else a, array)


def from_partner(block, axis, apart):
    count = lax.axis_size(axis)
    route = []
    for low in range(count):
        high = low | 1 << apart
        if high != low and high < count:
            route += [(low, high), (high, low)]
    return lax.ppermute(block, axis, route)


def best_against(best, mine, other):
    mine_unit, mine_cluster, mine_rank = mine
    other_unit, other_cluster, other_rank = other
    query_total = mine_unit.shape[0]
    key_total = other_unit.shape[0]
    query_size = min(512, query_total)
    key_size = min(512, key_total)

    def query_block(query_index, current_best):
        query_start = query_index * query_size
        query_unit = lax.dynamic_slice_in_dim(mine_unit, query_start, query_size, 0)
        query_cluster = lax.dynamic_slice_in_dim(mine_cluster, query_start, query_size, 0)
        query_rank = lax.dynamic_slice_in_dim(mine_rank, query_start, query_size, 0)
        running = lax.dynamic_slice_in_dim(current_best, query_start, query_size, 0)

        def key_block(key_index, running_best):
            key_start = key_index * key_size
            key_unit = lax.dynamic_slice_in_dim(other_unit, key_start, key_size, 0)
            key_cluster = lax.dynamic_slice_in_dim(other_cluster, key_start, key_size, 0)
            key_rank = lax.dynamic_slice_in_dim(other_rank, key_start, key_size, 0)
            allowed = (key_cluster[None, :] == query_cluster[:, None]) & (key_cluster[None, :] >= 0)
            allowed = allowed & (key_rank[None, :] < query_rank[:, None])
            scores = jnp.einsum(
                "qd,kd->qk", query_unit, key_unit, preferred_element_type=jnp.float32
            )
            return jnp.maximum(
                running_best, jnp.max(jnp.where(allowed, scores, jnp.float32(-1.0)), axis=1)
            )

        running = lax.fori_loop(0, key_total // key_size, key_block, running)
        return lax.dynamic_update_slice_in_dim(current_best, running, query_start, 0)

    return lax.fori_loop(0, query_total // query_size, query_block, best)


def route_rows(embeds, clusters, ranks):
    count = lax.axis_size("owner")
    rows, width = embeds.shape
    slots = max(2, 2 * rows // count)
    total = count * slots
    large_cap = total
    values = embeds.astype(jnp.float32)
    unit = (values * lax.rsqrt(jnp.sum(values * values, axis=1, keepdims=True) + 1e-06)).astype(
        jnp.bfloat16
    )
    is_large = clusters >= count
    target = jnp.where(is_large, 8 * (clusters - count) + ranks % 8, clusters)
    positions = jnp.arange(rows, dtype=jnp.int32)
    later = positions[:, None] > positions[None, :]
    earlier = (target[:, None] == target[None, :]) & later
    place = target * slots + jnp.sum(earlier.astype(jnp.int32), axis=1)
    send_unit = jnp.zeros((total, width), jnp.bfloat16).at[place].set(unit)
    send_cluster = jnp.full((total,), -1, jnp.int32).at[place].set(clusters)
    send_rank = jnp.zeros((total,), jnp.int32).at[place].set(ranks)
    got_unit, got_cluster, got_rank = (
        lax.all_to_all(
            send_unit.reshape(count, slots, width), "owner", split_axis=0, concat_axis=0, tiled=True
        ),
        lax.all_to_all(
            send_cluster.reshape(count, slots), "owner", split_axis=0, concat_axis=0, tiled=True
        ),
        lax.all_to_all(
            send_rank.reshape(count, slots), "owner", split_axis=0, concat_axis=0, tiled=True
        ),
    )
    mine = (got_unit.reshape(total, width), got_cluster.reshape(total), got_rank.reshape(total))
    best = jnp.full((total,), -1.0, jnp.float32)
    best = best_against(best, mine, mine)
    large_slot = mine[1] >= count
    large_position = jnp.cumsum(large_slot.astype(jnp.int32)) - 1
    large_place = jnp.where(large_slot, large_position, large_cap)
    large = (
        jnp.zeros((large_cap, width), jnp.bfloat16).at[large_place].set(mine[0], mode="drop"),
        jnp.full((large_cap,), -1, jnp.int32).at[large_place].set(mine[1], mode="drop"),
        jnp.zeros((large_cap,), jnp.int32).at[large_place].set(mine[2], mode="drop"),
    )
    large_best = jnp.full((large_cap,), -1.0, jnp.float32)
    gathered = large
    for level in range(3):
        partner = jax.tree.map(
            lambda part, own: part.astype(own.dtype),
            from_partner(as_sent(gathered), "owner", level),
            gathered,
        )
        large_best = best_against(large_best, large, partner)
        if level < 2:
            gathered = jax.tree.map(
                lambda left, right: jnp.concatenate([left, right], axis=0), gathered, partner
            )
    picked = large_best[jnp.clip(large_position, 0, large_cap - 1)]
    best = jnp.where(large_slot, jnp.maximum(best, picked), best)
    returned = lax.all_to_all(
        best.reshape(count, slots), "owner", split_axis=0, concat_axis=0, tiled=True
    )
    return returned.reshape(total)[place]


def local(embeds, clusters, ranks):
    if lax.axis_size("owner") != OWNERS:
        return route_rows(embeds, clusters, ranks)
    best, over = meet(embeds, clusters, ranks)
    return lax.cond(over, lambda *args: route_rows(*args[:3]), lambda *args: args[3],
                    embeds, clusters, ranks, best)


def solution(mesh):
    return jax.shard_map(
        local,
        mesh=mesh,
        in_specs=(P(("groups", "owner"), None), P(("groups", "owner")), P(("groups", "owner"))),
        out_specs=P(("groups", "owner")),
        check_vma=False,
    )
```

```python
import functools

import jax
import jax.numpy as jnp
from jax import lax
from jax.experimental import pallas as pl
from jax.experimental.pallas import tpu as pltpu
from jax.sharding import PartitionSpec as P

OWNERS = 16
CHIPS = 8
HOMES = (2, 3, 4, 5)
HOME_ROUNDS = (0, 6)
OUTER_ROUNDS = (2, 4)
ORDER = (2, 6, 0, 4)
BLOCK = 160
CAP = 156
META = 16
HELD = CHIPS * BLOCK
VMEM_LIMIT = 28 * 1024 * 1024
NT = (((1,), (1,)), ((), ()))


def is_home(chip):
    return (chip >= HOMES[0]) & (chip <= HOMES[-1])


def pack_rows(unit_ref, meta_ref, slot_ref, chip, to_core, out_ref):
    rows = slot_ref.shape[1]
    first = META - (BLOCK - CAP)
    place = lax.broadcasted_iota(jnp.int32, (256, rows), 0)
    over = (jnp.max(slot_ref[...]) >= CAP).astype(jnp.float32)
    for n in range(2):
        at = n * BLOCK
        k = jnp.where(is_home(chip), HOME_ROUNDS[n], OUTER_ROUNDS[n]) | to_core
        mine = slot_ref[pl.ds((chip ^ k) - HOMES[0], 1), :]
        hot = ((place == mine) & (place < CAP)).astype(jnp.float32).astype(jnp.bfloat16)
        block = jnp.dot(hot[:BLOCK], unit_ref[...], preferred_element_type=jnp.float32)
        out_ref[at : at + BLOCK] = block.astype(jnp.bfloat16)
        tail = lax.dot_general(meta_ref[...], hot, NT, preferred_element_type=jnp.float32)
        row = lax.broadcasted_iota(jnp.int32, (META, 256), 0)
        tail = jnp.where(row == META - 1, over, tail)
        tail = jnp.where(row >= first, tail, block[BLOCK - META :, :256])
        out_ref[at + BLOCK - META : at + BLOCK, :256] = tail.astype(jnp.bfloat16)


def pack_kernel(x_ref, cluster_ref, rank_ref, give_ref, slot_ref, unit_ref, meta_ref):
    me = lax.axis_index("owner")
    chip = me // 2
    core = me % 2
    values = x_ref[...].astype(jnp.float32)
    unit = (values * lax.rsqrt(jnp.sum(values * values, axis=1, keepdims=True) + 1e-06)).astype(
        jnp.bfloat16
    )
    rows, width = unit.shape
    cluster = cluster_ref[...]
    rank = rank_ref[...]
    home = jnp.where(
        cluster < OWNERS // 2,
        3,
        jnp.where(cluster < OWNERS, 4, jnp.where(cluster == OWNERS, 2, 5)),
    )
    number = lax.broadcasted_iota(jnp.int32, (8, rows), 0)
    member = number + HOMES[0] == home
    upper = (
        lax.broadcasted_iota(jnp.int32, (rows, rows), 0)
        < lax.broadcasted_iota(jnp.int32, (rows, rows), 1)
    ).astype(jnp.float32).astype(jnp.bfloat16)
    before = jnp.dot(
        member.astype(jnp.float32).astype(jnp.bfloat16), upper, preferred_element_type=jnp.float32
    )
    slot = jnp.where(member, before.astype(jnp.int32), -1)
    slot_ref[...] = slot
    line = lax.broadcasted_iota(jnp.int32, (META, rows), 0)
    first = META - (BLOCK - CAP)
    meta = jnp.where(
        line == first,
        cluster + 1,
        jnp.where(line == first + 1, rank >> 6, jnp.where(line == first + 2, rank & 63, 0)),
    )
    meta = meta.astype(jnp.float32).astype(jnp.bfloat16)
    unit_ref[...] = unit
    meta_ref[...] = meta
    pack_rows(unit_ref, meta_ref, slot_ref, chip, core ^ 1, give_ref)


def keep_kernel(unit_ref, meta_ref, slot_ref, keep_ref):
    me = lax.axis_index("owner")
    pack_rows(unit_ref, meta_ref, slot_ref, me // 2, me % 2, keep_ref)


def fill_codes(keys, codes, blocks):
    eye = (
        lax.broadcasted_iota(jnp.int32, (BLOCK, 256), 0)
        == lax.broadcasted_iota(jnp.int32, (BLOCK, 256), 1)
    ).astype(jnp.float32).astype(jnp.bfloat16)
    lane = lax.broadcasted_iota(jnp.int32, (1, META), 1)
    first = META - (BLOCK - CAP)
    scale = jnp.where(
        lane == first, 4096.0, jnp.where(lane == first + 1, 64.0, jnp.where(lane == first + 2, 1.0, 0.0))
    )
    over = jnp.zeros((1, 128), jnp.float32)
    for n in range(blocks):
        meta = keys[(n + 1) * BLOCK - META : (n + 1) * BLOCK, :256]
        over = jnp.maximum(over, meta[META - 1 :, :128].astype(jnp.float32))
        columns = lax.dot_general(eye, meta, NT, preferred_element_type=jnp.float32)
        code = jnp.sum(columns * scale, axis=1, keepdims=True)
        codes[n * BLOCK : (n + 1) * BLOCK] = jnp.broadcast_to(code, (BLOCK, 128))
    return over


def best_of(keys, codes, query, top, first=0):
    size = query.shape[0]
    total = keys.shape[0]
    step = (total - first) // 2
    base = jnp.floor(top * (1.0 / 4096.0)) * 4096.0
    best = jnp.full((8, size), -1.0, jnp.float32)
    for start in range(first, total, step):
        score = lax.dot_general(
            keys[start : start + step], query, NT, preferred_element_type=jnp.float32
        )
        code = jnp.concatenate([codes[start : start + step]] * (size // 128), axis=1)
        score = jnp.where((code >= base) & (code < top), score, -1.0)
        best = jnp.maximum(best, jnp.max(score.reshape(step // 8, 8, size), axis=0))
    return best


def pair_kernel(keep_ref, got_ref, first_ref, second_ref):
    first_ref[:BLOCK] = keep_ref[:BLOCK]
    first_ref[BLOCK:] = got_ref[:BLOCK]
    second_ref[:BLOCK] = keep_ref[BLOCK:]
    second_ref[BLOCK:] = got_ref[BLOCK:]


def halve_kernel(pair_ref, one_ref, two_ref):
    one_ref[...] = pair_ref[:BLOCK]
    two_ref[...] = pair_ref[BLOCK:]


def early_kernel(pair_ref, one_ref, two_ref, best_ref, keys, codes):
    @pl.when(is_home(lax.axis_index("owner") // 2))
    def _():
        keys[: 2 * BLOCK] = pair_ref[...]
        keys[2 * BLOCK : 3 * BLOCK] = one_ref[...]
        keys[3 * BLOCK :] = two_ref[...]
        fill_codes(keys, codes, 4)
        top = jnp.transpose(codes[:256])[:1]
        best_ref[...] = best_of(keys, codes, keys[:256], top)


def join_kernel(mine_ref, one_ref, two_ref, early_ref, *refs):
    blocks, (out_ref, late_ref, known_ref) = refs[:-3], refs[-3:]
    known_ref[...] = early_ref[...]
    for n, ref in enumerate(blocks):
        out_ref[n * 2 * BLOCK : (n + 1) * 2 * BLOCK] = ref[...]

    @pl.when(lax.axis_index("owner") % 2 == 0)
    def _():
        at = ORDER.index(0) * 2 * BLOCK
        out_ref[at : at + 2 * BLOCK] = mine_ref[...]

    out_ref[HELD : HELD + BLOCK] = one_ref[...]
    out_ref[HELD + BLOCK :] = two_ref[...]
    late_ref[...] = out_ref[2 * BLOCK : HELD]


def own_kernel(mine_ref, early_ref, late_ref, best_ref, top_ref, over_ref, codes):
    @pl.when(is_home(lax.axis_index("owner") // 2))
    def _():
        over_ref[...] = jnp.broadcast_to(fill_codes(mine_ref, codes, CHIPS + 2), over_ref.shape)
        late_codes = codes.at[pl.ds(2 * BLOCK, HELD - 2 * BLOCK)]
        for at in range(0, HELD, 256):
            top = jnp.transpose(codes[at : at + 256])[:8]
            top_ref[:, at : at + 256] = top
            if at == 0:
                own = best_of(late_ref, late_codes, mine_ref[:256], top[:1])
                best_ref[:, :256] = jnp.maximum(early_ref[...], own)
            else:
                best_ref[:, at : at + 256] = best_of(
                    mine_ref, codes, mine_ref[at : at + 256], top[:1]
                )


def other_kernel(mine_ref, other_ref, best_ref, top_ref, over_ref, out_ref, codes):
    me = lax.axis_index("owner")
    chip = me // 2
    core = me % 2

    @pl.when(is_home(chip))
    def _():
        over = jnp.max(jnp.maximum(fill_codes(other_ref, codes, CHIPS - 2), over_ref[:1]))
        found = [
            jnp.maximum(
                best_ref[:, at : at + 256],
                best_of(other_ref, codes, mine_ref[at : at + 256], top_ref[:1, at : at + 256]),
            )
            for at in range(0, HELD, 256)
        ]
        found = jnp.max(jnp.concatenate(found, axis=1), axis=0, keepdims=True)
        found = jnp.broadcast_to(found, (8, HELD))
        lane = lax.broadcasted_iota(jnp.int32, (1, 128), 1)
        for n in range(CHIPS):
            start = n * BLOCK
            to_chip = chip ^ (ORDER[n // 2] | core)
            to_core = core ^ (n % 2)
            base = min(start // 128 * 128, HELD - 256)
            size = min(384, HELD - base)
            part = found[:, base : base + size]
            if start > base:
                part = pltpu.roll(part, size - (start - base), 1)
            row = 8 * (2 * to_chip + to_core)
            out_ref[pl.ds(row, 1), :] = part[:1, :128]
            out_ref[pl.ds(row + 1, 1), :] = jnp.where(lane >= CAP - 128, over, part[:1, 128:256])


def unpack_kernel(back_ref, slot_ref, best_ref, over_ref):
    chip = lax.axis_index("owner") // 2
    rows = slot_ref.shape[1]
    place = lax.broadcasted_iota(jnp.int32, (128, rows), 0)
    row = lax.broadcasted_iota(jnp.int32, (8, 128), 0)
    total = jnp.zeros((8, rows), jnp.float32)
    over = jnp.zeros((8, 128), jnp.float32)
    for n, home in enumerate(HOMES):
        held = 2 * home + ((chip ^ home) & 1)
        part = back_ref[pl.ds(pl.multiple_of(8 * held, 8), 8), :]
        over = jnp.maximum(over, part)
        for half in range(2):
            value = part[half : half + 1]
            high = value.astype(jnp.bfloat16).astype(jnp.float32)
            middle = (value - high).astype(jnp.bfloat16).astype(jnp.float32)
            low = value - high - middle
            split = jnp.where(row == 0, high, jnp.where(row == 1, middle, jnp.where(row == 2, low, 0.0)))
            hot = (place + 128 * half == slot_ref[n : n + 1]) & (place + 128 * half < BLOCK)
            total = total + jnp.dot(
                split.astype(jnp.bfloat16),
                hot.astype(jnp.float32).astype(jnp.bfloat16),
                preferred_element_type=jnp.float32,
            )
    best_ref[...] = jnp.sum(total, axis=0, keepdims=True)
    over_ref[0, 0] = (over[1, BLOCK - 1 - 128] > 0.0).astype(jnp.int32)


def meet(embeds, clusters, ranks):
    rows, width = embeds.shape
    vmem = pl.BlockSpec(memory_space=pltpu.VMEM)
    params = pltpu.CompilerParams(vmem_limit_bytes=VMEM_LIMIT)
    two_blocks = jax.ShapeDtypeStruct((2 * BLOCK, width), jnp.bfloat16)
    give, slot, unit, meta = pl.pallas_call(
        pack_kernel,
        out_shape=[
            two_blocks,
            jax.ShapeDtypeStruct((8, rows), jnp.int32),
            jax.ShapeDtypeStruct((rows, width), jnp.bfloat16),
            jax.ShapeDtypeStruct((META, rows), jnp.bfloat16),
        ],
        in_specs=[vmem] * 3,
        out_specs=[vmem] * 4,
        compiler_params=params,
        name="pack",
    )(embeds, clusters.reshape(1, rows), ranks.reshape(1, rows))
    got = lax.ppermute(give, "owner", [(n, n ^ 1) for n in range(OWNERS)])
    keep = pl.pallas_call(
        keep_kernel,
        out_shape=two_blocks,
        in_specs=[vmem] * 3,
        out_specs=vmem,
        compiler_params=params,
        cost_estimate=pl.CostEstimate(
            flops=4 * BLOCK * rows * width, bytes_accessed=4 * rows * width, transcendentals=0
        ),
        name="keep",
    )(unit, meta, slot)
    first, second = pl.pallas_call(
        pair_kernel,
        out_shape=[two_blocks] * 2,
        in_specs=[vmem] * 2,
        out_specs=[vmem] * 2,
        compiler_params=params,
        name="pair",
    )(keep, got)

    def carry(pair, k, cores=(0, 1)):
        chips = [s for s in range(CHIPS) if (s in HOMES) == (k in HOME_ROUNDS)]
        return lax.ppermute(
            pair, "owner", [(2 * s + c, 2 * (s ^ (k | c)) + c) for s in chips for c in cores]
        )

    pairs = {6: carry(second, 6), 4: carry(second, 4), 2: carry(first, 2), 0: carry(first, 0, (1,))}
    swap = [(2 * h + c, 2 * h + 1 - c) for h in HOMES for c in range(2)]
    line = jax.ShapeDtypeStruct((8, HELD), jnp.float32)
    codes = [pltpu.VMEM((HELD + 2 * BLOCK, 128), jnp.float32)]
    cost = pl.CostEstimate(
        flops=2 * HELD * HELD * width, bytes_accessed=2 * HELD * width, transcendentals=0
    )
    halves = pl.pallas_call(
        halve_kernel,
        out_shape=[jax.ShapeDtypeStruct((BLOCK, width), jnp.bfloat16)] * 2,
        in_specs=[vmem],
        out_specs=[vmem] * 2,
        compiler_params=params,
        name="halve",
    )(pairs[2])
    halves = [lax.ppermute(block, "owner", swap) for block in halves]
    early = pl.pallas_call(
        early_kernel,
        out_shape=jax.ShapeDtypeStruct((8, 256), jnp.float32),
        in_specs=[vmem] * 3,
        out_specs=vmem,
        scratch_shapes=[
            pltpu.VMEM((4 * BLOCK, width), jnp.bfloat16),
            pltpu.VMEM((4 * BLOCK, 128), jnp.float32),
        ],
        compiler_params=params,
        cost_estimate=pl.CostEstimate(flops=0, bytes_accessed=0, transcendentals=0),
        name="early",
    )(pairs[2], *halves)
    mine, late, early = pl.pallas_call(
        join_kernel,
        out_shape=[
            jax.ShapeDtypeStruct((HELD + 2 * BLOCK, width), jnp.bfloat16),
            jax.ShapeDtypeStruct((HELD - 2 * BLOCK, width), jnp.bfloat16),
            jax.ShapeDtypeStruct((8, 256), jnp.float32),
        ],
        in_specs=[vmem] * (4 + len(ORDER)),
        out_specs=[vmem] * 3,
        compiler_params=params,
        name="join",
    )(first, *halves, early, *[pairs[k] for k in ORDER])
    other = lax.ppermute(late, "owner", swap)
    best, top, over = pl.pallas_call(
        own_kernel,
        out_shape=[line, line, jax.ShapeDtypeStruct((8, 128), jnp.float32)],
        in_specs=[vmem] * 3,
        out_specs=[vmem] * 3,
        scratch_shapes=codes,
        compiler_params=params,
        cost_estimate=cost,
        name="own",
    )(mine, early, late)
    found = pl.pallas_call(
        other_kernel,
        out_shape=jax.ShapeDtypeStruct((8 * OWNERS, 128), jnp.float32),
        in_specs=[vmem] * 5,
        out_specs=vmem,
        scratch_shapes=codes,
        compiler_params=params,
        cost_estimate=cost,
        name="other",
    )(mine, other, best, top, over)
    back = lax.all_to_all(
        found.reshape(OWNERS, 8, 128), "owner", split_axis=0, concat_axis=0, tiled=True
    )
    best, over = pl.pallas_call(
        unpack_kernel,
        out_shape=[
            jax.ShapeDtypeStruct((1, rows), jnp.float32),
            jax.ShapeDtypeStruct((1, 1), jnp.int32),
        ],
        in_specs=[vmem] * 2,
        out_specs=[vmem, pl.BlockSpec(memory_space=pltpu.SMEM)],
        compiler_params=params,
        name="unpack",
    )(back.reshape(8 * OWNERS, 128), slot)
    return best.reshape(rows), over[0, 0] > 0


def as_sent(array):
    return jax.tree.map(lambda a: a.astype(jnp.bfloat16) if a.dtype == jnp.float32 else a, array)


def from_partner(block, axis, apart):
    count = lax.axis_size(axis)
    route = []
    for low in range(count):
        high = low | 1 << apart
        if high != low and high < count:
            route += [(low, high), (high, low)]
    return lax.ppermute(block, axis, route)


def best_against(best, mine, other):
    mine_unit, mine_cluster, mine_rank = mine
    other_unit, other_cluster, other_rank = other
    query_total = mine_unit.shape[0]
    key_total = other_unit.shape[0]
    query_size = min(512, query_total)
    key_size = min(512, key_total)

    def query_block(query_index, current_best):
        query_start = query_index * query_size
        query_unit = lax.dynamic_slice_in_dim(mine_unit, query_start, query_size, 0)
        query_cluster = lax.dynamic_slice_in_dim(mine_cluster, query_start, query_size, 0)
        query_rank = lax.dynamic_slice_in_dim(mine_rank, query_start, query_size, 0)
        running = lax.dynamic_slice_in_dim(current_best, query_start, query_size, 0)

        def key_block(key_index, running_best):
            key_start = key_index * key_size
            key_unit = lax.dynamic_slice_in_dim(other_unit, key_start, key_size, 0)
            key_cluster = lax.dynamic_slice_in_dim(other_cluster, key_start, key_size, 0)
            key_rank = lax.dynamic_slice_in_dim(other_rank, key_start, key_size, 0)
            allowed = (key_cluster[None, :] == query_cluster[:, None]) & (key_cluster[None, :] >= 0)
            allowed = allowed & (key_rank[None, :] < query_rank[:, None])
            scores = jnp.einsum(
                "qd,kd->qk", query_unit, key_unit, preferred_element_type=jnp.float32
            )
            return jnp.maximum(
                running_best, jnp.max(jnp.where(allowed, scores, jnp.float32(-1.0)), axis=1)
            )

        running = lax.fori_loop(0, key_total // key_size, key_block, running)
        return lax.dynamic_update_slice_in_dim(current_best, running, query_start, 0)

    return lax.fori_loop(0, query_total // query_size, query_block, best)


def route_rows(embeds, clusters, ranks):
    count = lax.axis_size("owner")
    rows, width = embeds.shape
    slots = max(2, 2 * rows // count)
    total = count * slots
    large_cap = total
    values = embeds.astype(jnp.float32)
    unit = (values * lax.rsqrt(jnp.sum(values * values, axis=1, keepdims=True) + 1e-06)).astype(
        jnp.bfloat16
    )
    is_large = clusters >= count
    target = jnp.where(is_large, 8 * (clusters - count) + ranks % 8, clusters)
    positions = jnp.arange(rows, dtype=jnp.int32)
    later = positions[:, None] > positions[None, :]
    earlier = (target[:, None] == target[None, :]) & later
    place = target * slots + jnp.sum(earlier.astype(jnp.int32), axis=1)
    send_unit = jnp.zeros((total, width), jnp.bfloat16).at[place].set(unit)
    send_cluster = jnp.full((total,), -1, jnp.int32).at[place].set(clusters)
    send_rank = jnp.zeros((total,), jnp.int32).at[place].set(ranks)
    got_unit, got_cluster, got_rank = (
        lax.all_to_all(
            send_unit.reshape(count, slots, width), "owner", split_axis=0, concat_axis=0, tiled=True
        ),
        lax.all_to_all(
            send_cluster.reshape(count, slots), "owner", split_axis=0, concat_axis=0, tiled=True
        ),
        lax.all_to_all(
            send_rank.reshape(count, slots), "owner", split_axis=0, concat_axis=0, tiled=True
        ),
    )
    mine = (got_unit.reshape(total, width), got_cluster.reshape(total), got_rank.reshape(total))
    best = jnp.full((total,), -1.0, jnp.float32)
    best = best_against(best, mine, mine)
    large_slot = mine[1] >= count
    large_position = jnp.cumsum(large_slot.astype(jnp.int32)) - 1
    large_place = jnp.where(large_slot, large_position, large_cap)
    large = (
        jnp.zeros((large_cap, width), jnp.bfloat16).at[large_place].set(mine[0], mode="drop"),
        jnp.full((large_cap,), -1, jnp.int32).at[large_place].set(mine[1], mode="drop"),
        jnp.zeros((large_cap,), jnp.int32).at[large_place].set(mine[2], mode="drop"),
    )
    large_best = jnp.full((large_cap,), -1.0, jnp.float32)
    gathered = large
    for level in range(3):
        partner = jax.tree.map(
            lambda part, own: part.astype(own.dtype),
            from_partner(as_sent(gathered), "owner", level),
            gathered,
        )
        large_best = best_against(large_best, large, partner)
        if level < 2:
            gathered = jax.tree.map(
                lambda left, right: jnp.concatenate([left, right], axis=0), gathered, partner
            )
    picked = large_best[jnp.clip(large_position, 0, large_cap - 1)]
    best = jnp.where(large_slot, jnp.maximum(best, picked), best)
    returned = lax.all_to_all(
        best.reshape(count, slots), "owner", split_axis=0, concat_axis=0, tiled=True
    )
    return returned.reshape(total)[place]


def local(embeds, clusters, ranks):
    if lax.axis_size("owner") != OWNERS:
        return route_rows(embeds, clusters, ranks)
    best, over = meet(embeds, clusters, ranks)
    return lax.cond(over, lambda *args: route_rows(*args[:3]), lambda *args: args[3],
                    embeds, clusters, ranks, best)


def solution(mesh):
    return jax.shard_map(
        local,
        mesh=mesh,
        in_specs=(P(("groups", "owner"), None), P(("groups", "owner")), P(("groups", "owner"))),
        out_specs=P(("groups", "owner")),
        check_vma=False,
    )
```
